32 devices in a mesh: circ: 16 (over z, y, core), mode: 2 (over x).
Axes of the slice: x: 2, y: 2, z: 4, core: 2. Of those that a mesh axis runs over, the one named last changes fastest.
Arguments:
- right_side: float32 [20, 3, 32, 1024], P('mode', None, 'circ'), may hold values from -5 to 5
- stiffness: float32 [4, 32, 1024], P(None, 'circ'), may hold values from -0.15 to 2, as said below
- pairing: int32 [3, 20], replicated, may hold values from 0 to 19, each once within a row
- coupling: float32 [3, 20], replicated, may hold values from -1 to 1
Outputs:
- solution_field: float32 [20, 3, 32, 1024], P('mode', None, 'circ')
- residual: float32 [20, 3, 32, 1024], P('mode', None, 'circ')
The draws below stay inside these ranges and needn't reach their ends.
Inputs may be any that keep to these rules, and one draw needn't show every extreme that they name: `pairing`: each row is a permutation of the 20 chaos modes. The mean stiffness lies in [1, 2], the three random modes in [-0.15, 0.15].
All inputs are finite; a program needn't handle non-finite values.
Results may differ from the reference program's by a relative error of at most 0.001.
Values sent between devices are 32-bit elements; how exact they have to be, the bound alone decides.
No kernel may reach another device: no remote copies, remote signals or barrier semaphores. Data moves between devices by JAX's collectives and lax.ppermute only.
A program may use at most 64 MiB of HBM per device.

```python
import math
import jax
import jax.numpy as jnp
from jax import lax

P_SIZE = 20
KM = 4
NL = 16
NT = 64
ITERS = 2
NC = 32


def draw_stiffness(key, part):
    key_mean = jax.random.fold_in(key, 11)
    key_pert = jax.random.fold_in(key, 12)
    mean_part = jax.random.uniform(key_mean, (1, NC, NL * NT), jnp.float32, 1.0, 2.0)
    pert_part = jax.random.uniform(key_pert, (KM - 1, NC, NL * NT), jnp.float32, -0.15, 0.15)
    return jnp.concatenate([mean_part, pert_part], 0)


def draw_right_side(key, part):
    key_main = jax.random.fold_in(key, 21)
    mode_ids = jnp.arange(P_SIZE, dtype=jnp.int32)
    mode_scale = jnp.where(mode_ids < P_SIZE // 2, 1.0, 0.1).astype(jnp.float32)[:, None, None, None]
    rough = jax.random.normal(key_main, (P_SIZE, 3, NC, NL * NT), jnp.float32)
    return mode_scale * jnp.clip(rough, -5.0, 5.0)


def setup_inputs(seed: int = 0) -> dict:
    seeds = jax.random.split(jax.random.key(seed), 5)
    return {
        "right_side": draw_right_side(jax.random.fold_in(seeds[4], 71), 0),
        "stiffness": draw_stiffness(jax.random.fold_in(seeds[4], 71), 0),
        "pairing": jax.vmap(lambda own: jax.random.permutation(own, P_SIZE))(jax.random.split(seeds[2], (KM - 1))).reshape((KM - 1, P_SIZE)).astype(jnp.int32),
        "coupling": jnp.clip(jax.random.uniform(seeds[3], (KM - 1, P_SIZE), jnp.float32, -1.0, 1.0), -1.0, 1.0),
    }


LAME_RATIO = 1.0


def dir_weight(component, direction):
    return 1.0 + LAME_RATIO if component == direction else 1.0


def weight_column(direction, trailing):
    values = jnp.array([dir_weight(comp_no, direction) for comp_no in range(3)], jnp.float32)
    return values.reshape((3,) + (1,) * trailing)


def stencil(padded, coeff_pad, n_long, n_trans):
    num_modes, num_comps, span_pad, num_cells = padded.shape
    span = span_pad - 2
    center = padded[:, :, 1:-1]
    coeff_mid = coeff_pad[1:-1]
    right_face = 0.5 * (coeff_mid + coeff_pad[2:])
    left_face = 0.5 * (coeff_mid + coeff_pad[:-2])
    circ_part = right_face * (center - padded[:, :, 2:]) + left_face * (center - padded[:, :, :-2])
    field = center.reshape(num_modes, num_comps, span, n_long, n_trans)
    coeff_cube = coeff_mid.reshape(span, n_long, n_trans)
    long_face = 0.5 * (coeff_cube[:, :-1] + coeff_cube[:, 1:])
    long_flux = long_face * (field[:, :, :, 1:] - field[:, :, :, :-1])
    zero_row = jnp.zeros((num_modes, num_comps, span, 1, n_trans), jnp.float32)
    long_part = jnp.concatenate([zero_row, long_flux], 3) - jnp.concatenate([long_flux, zero_row], 3)
    edge_pad = jnp.pad(coeff_cube, ((0, 0), (0, 0), (1, 1)), mode="edge")
    trans_face = 0.5 * (edge_pad[:, :, :-1] + edge_pad[:, :, 1:])
    zero_pad = jnp.pad(field, ((0, 0), (0, 0), (0, 0), (0, 0), (1, 1)))
    trans_flux = trans_face * (zero_pad[..., 1:] - zero_pad[..., :-1])
    trans_part = trans_flux[..., :-1] - trans_flux[..., 1:]
    inner = weight_column(1, 3) * long_part + weight_column(2, 3) * trans_part
    return weight_column(0, 2) * circ_part + inner.reshape(num_modes, num_comps, span, num_cells)


def build_coupling(pairing, coupling):
    modes = pairing.shape[1]
    onehot = (pairing[:, :, None] == jnp.arange(modes, dtype=jnp.int32)[None, None, :]).astype(jnp.float32)
    halfway = coupling[:, :, None] * onehot
    return 0.5 * (halfway + jnp.swapaxes(halfway, 1, 2))


def hartley_table(size):
    indices = jnp.arange(size, dtype=jnp.int32)
    product = (indices[:, None] * indices[None, :]) % size
    angle = (2.0 * math.pi / size) * product.astype(jnp.float32)
    return jnp.cos(angle) + jnp.sin(angle)


def cosine_table(size):
    indices = jnp.arange(size, dtype=jnp.int32)
    product = ((2 * indices[:, None] + 1) * indices[None, :]) % (4 * size)
    return jnp.cos((math.pi / (2 * size)) * product.astype(jnp.float32))


def sine_table(size):
    indices = jnp.arange(size, dtype=jnp.int32) + 1
    product = (indices[:, None] * indices[None, :]) % (2 * (size + 1))
    return jnp.sin((math.pi / (size + 1)) * product.astype(jnp.float32))


def eigen_denominator(freq_circ, freq_long, freq_trans, n_circ, n_long, n_trans):
    lam_circ = 2.0 - 2.0 * jnp.cos((2.0 * math.pi / n_circ) * freq_circ.astype(jnp.float32))
    lam_long = 2.0 - 2.0 * jnp.cos((math.pi / n_long) * freq_long.astype(jnp.float32))
    lam_trans = 2.0 - 2.0 * jnp.cos((math.pi / (n_trans + 1)) * (freq_trans + 1).astype(jnp.float32))
    norm_long = jnp.where(freq_long == 0, 1.0 * n_long, 0.5 * n_long).astype(jnp.float32)
    scale = n_circ * norm_long * (0.5 * (n_trans + 1))
    rows = []
    for comp_no in range(3):
        lam = dir_weight(comp_no, 0) * lam_circ + dir_weight(comp_no, 1) * lam_long + dir_weight(comp_no, 2) * lam_trans
        rows.append(lam * scale)
    return jnp.stack(rows, 0)


def precondition(values):
    num_modes, num_comps, n_circ, num_cells = values.shape
    htab = hartley_table(n_circ)
    ctab = cosine_table(NL)
    stab = sine_table(NT)
    freq_circ = jnp.arange(n_circ, dtype=jnp.int32)[:, None, None]
    freq_long = jnp.arange(NL, dtype=jnp.int32)[None, :, None]
    freq_trans = jnp.arange(NT, dtype=jnp.int32)[None, None, :]
    denom = eigen_denominator(freq_circ, freq_long, freq_trans, n_circ, NL, NT)
    hp = lax.Precision.HIGHEST
    field = values.reshape(num_modes, num_comps, n_circ, NL, NT)
    spec = jnp.einsum("pcnlt,lm->pcnmt", field, ctab, precision=hp)
    spec = jnp.einsum("pcnmt,ts->pcnms", spec, stab, precision=hp)
    spec = jnp.einsum("pcnms,nk->pckms", spec, htab, precision=hp)
    spec = spec / denom[None]
    spec = jnp.einsum("pckms,kn->pcnms", spec, htab, precision=hp)
    spec = jnp.einsum("pcnms,lm->pcnls", spec, ctab, precision=hp)
    spec = jnp.einsum("pcnls,ts->pcnlt", spec, stab, precision=hp)
    return spec.reshape(num_modes, num_comps, n_circ, num_cells)


def apply_operator(values, stiffness, gmat):
    padded = jnp.concatenate([values[:, :, -1:], values, values[:, :, :1]], 2)
    coeff_pad = jnp.concatenate([stiffness[:, -1:], stiffness, stiffness[:, :1]], 1)
    result = stencil(padded, coeff_pad[0], NL, NT)
    for order in range(1, KM):
        term = stencil(padded, coeff_pad[order], NL, NT)
        result = result + jnp.einsum("ij,jcnq->icnq", gmat[order - 1], term, precision=lax.Precision.HIGHEST)
    return result


def reference(right_side, stiffness, pairing, coupling):
    gmat = build_coupling(pairing, coupling)
    solution_field = jnp.zeros_like(right_side)
    residual = right_side
    smoothed = precondition(residual)
    direction = smoothed
    inner_now = jnp.sum(residual * smoothed)
    for iteration in range(ITERS):
        image = apply_operator(direction, stiffness, gmat)
        alpha = inner_now / jnp.sum(direction * image)
        solution_field = solution_field + alpha * direction
        residual = residual - alpha * image
        if iteration + 1 < ITERS:
            smoothed = precondition(residual)
            inner_next = jnp.sum(residual * smoothed)
            direction = smoothed + (inner_next / inner_now) * direction
            inner_now = inner_next
    return solution_field, residual
```

```python
import math

import jax
import jax.numpy as jnp
import numpy as np
from jax import lax
from jax.experimental import pallas as pl
from jax.experimental.pallas import tpu as pltpu
from jax.sharding import PartitionSpec as P

KM = 4
NL = 16
NT = 64
COMPS = 3
LANES = 2 * NT
HIGHEST = lax.Precision.HIGHEST

SHIFT = 2.0 / 3.0


def weight(comp, direction):
    return 2.0 if comp == direction else 1.0


def cosine_np():
    l = np.arange(NL)
    return np.cos(math.pi * l[None, :] * (2 * l[:, None] + 1) / (2 * NL))


def sine_np():
    t = np.arange(NT) + 1
    return np.sin(math.pi * t[:, None] * t[None, :] / (NT + 1))


def hartley_np(size):
    n = np.arange(size)
    angle = 2.0 * math.pi / size * (n[:, None] * n[None, :] % size)
    return np.cos(angle) + np.sin(angle)


def denominator_np(n_circ):
    lam_c = 2.0 - 2.0 * np.cos(2.0 * math.pi / n_circ * np.arange(n_circ))[:, None, None]
    lam_l = 2.0 - 2.0 * np.cos(math.pi / NL * np.arange(NL))[None, :, None]
    lam_t = 2.0 - 2.0 * np.cos(math.pi / (NT + 1) * (np.arange(NT) + 1))[None, None, :]
    norm = np.where(np.arange(NL) == 0, 1.0 * NL, 0.5 * NL)[None, :, None]
    rows = [weight(c, 0) * lam_c + weight(c, 1) * lam_l + weight(c, 2) * lam_t for c in range(COMPS)]
    return np.stack(rows) * (n_circ * norm * (0.5 * (NT + 1)))


COS = cosine_np()


def sine_pair():
    both = np.zeros((LANES, LANES))
    both[:NT, :NT] = sine_np()
    both[NT:, NT:] = sine_np()
    return both.astype(np.float32)


def circulant_table(n_circ):
    half = n_circ // 2
    quarter = half // 2
    freq = np.arange(n_circ)
    inverse = 1.0 / denominator_np(n_circ)
    turn = np.cos(2.0 * math.pi / n_circ * (freq[:, None] * freq[None, :] % n_circ))
    g = np.einsum("dk,ckms->dcms", turn, inverse)
    same = np.stack([np.concatenate([g[2 * d], g[2 * d]], -1) for d in range(half)])
    cross = np.stack(
        [np.concatenate([g[(2 * d - 1) % n_circ], g[(2 * d + 1) % n_circ]], -1) for d in range(half)]
    )
    parts = []
    for full in (same, cross):
        parts.append(0.5 * (full[:quarter] + full[quarter:]))
        parts.append(0.5 * (full[:quarter] - full[quarter:]))
    table = np.stack(parts)
    return np.transpose(table, (3, 0, 1, 2, 4)).astype(np.float32)


def whole():
    return pl.BlockSpec(memory_space=pltpu.VMEM)


def smem():
    return pl.BlockSpec(memory_space=pltpu.SMEM)


def params():
    return pltpu.CompilerParams(vmem_limit_bytes=32 * 1024 * 1024)


def forward_rows(load, sine_ref, out_ref, fields):
    for base in range(0, fields, 8):
        plus, minus = [], []
        for l in range(NL // 2):
            a, b = load(l, base), load(NL - 1 - l, base)
            plus.append(a + b)
            minus.append(a - b)
        for m in range(NL):
            src = plus if m % 2 == 0 else minus
            acc = src[0] * float(COS[0, m])
            for l in range(1, NL // 2):
                acc = acc + src[l] * float(COS[l, m])
            out_ref[m, base : base + 8, :] = acc
    flat = out_ref[...].reshape(NL * fields, LANES)
    done = jnp.dot(flat, sine_ref[...], precision=HIGHEST, preferred_element_type=jnp.float32)
    out_ref[...] = done.reshape(NL, fields, LANES)


def first_kernel(fields, b_ref, sine_ref, out_ref):
    forward_rows(lambda l, base: b_ref[pl.ds(base * NL + l, 8, stride=NL), :], sine_ref, out_ref, fields)


def next_kernel(fields, b_ref, own_ref, recv_ref, sine_ref, out_ref, image_ref, work_ref):
    image = own_ref[...] + recv_ref[...]
    image_ref[...] = image
    work_ref[...] = b_ref[...] - SHIFT * image
    forward_rows(lambda l, base: work_ref[pl.ds(base * NL + l, 8, stride=NL), :], sine_ref, out_ref, fields)


def circ_kernel(fields, half, x_ref, table_ref, out_ref):
    quarter = half // 2
    comp_row = lax.broadcasted_iota(jnp.int32, (8, LANES), 0)
    low = lax.broadcasted_iota(jnp.int32, (8, LANES), 1) < NT
    for base in range(0, fields, 8):
        comp = (comp_row + base) % COMPS

        def spread(part, d):
            rows = table_ref[part, d]
            return jnp.where(comp == 0, rows[0:1], jnp.where(comp == 1, rows[1:2], rows[2:3]))

        coef = [[spread(part, d) for d in range(quarter)] for part in range(4)]
        plus, minus, plus_x, minus_x = [], [], [], []
        for c in range(quarter):
            a = x_ref[c, base : base + 8, :]
            b = x_ref[c + quarter, base : base + 8, :]
            plus.append(a + b)
            minus.append(a - b)
            plus_x.append(pltpu.roll(a + b, NT, 1))
            minus_x.append(pltpu.roll(a - b, NT, 1))
        outs = [None] * half
        for c in range(quarter):
            even = odd = None
            for e in range(quarter):
                d = (c - e) % quarter
                term = coef[0][d] * plus[e] + coef[2][d] * plus_x[e]
                even = term if even is None else even + term
                term = coef[1][d] * minus[e] + coef[3][d] * minus_x[e]
                if c < e:
                    term = -term
                odd = term if odd is None else odd + term
            outs[c] = even + odd
            outs[c + quarter] = even - odd
        for c in range(half):
            out_ref[c, 0, base : base + 8, :] = outs[c]
            out_ref[c, 1, base : base + 8, :] = jnp.where(low, outs[(c + 1) % half], outs[c - 1])


def lane_masks(rows):
    lane = lax.broadcasted_iota(jnp.int32, (rows, LANES), 1)
    return lane < NT, lane % NT == 0, lane % NT == NT - 1


def neighbours(mid, ends, low):
    right = pltpu.roll(jnp.where(low, ends, mid), NT, 1)
    left = pltpu.roll(jnp.where(low, mid, ends), NT, 1)
    return right, left


def operator_kernel(
    modes, fields, row_ref, pair_ref, coup_ref, spec_ref, sine_ref, stiff_ref, stiff_l_ref, stiff_r_ref,
    field_ref, own_ref, cross_ref, work_ref, ends_ref, face_ref, term_ref, inv_ref
):
    total_modes = pair_ref.shape[1]
    low, first, last = lane_masks(NL)
    row = lax.broadcasted_iota(jnp.int32, (NL, LANES), 0)
    for k in range(KM):
        a = stiff_ref[k]
        ends = jnp.where(low, stiff_r_ref[k], stiff_l_ref[k])
        right, left = neighbours(a, ends, low)
        above = jnp.where(last, a, pltpu.roll(a, LANES - 1, 1))
        below = jnp.where(first, a, pltpu.roll(a, 1, 1))
        ahead = pltpu.roll(a, NL - 1, 0)
        behind = pltpu.roll(a, 1, 0)
        faces = [
            0.5 * (a + right),
            0.5 * (a + left),
            jnp.where(row == NL - 1, 0.0, 0.5 * (a + ahead)),
            jnp.where(row == 0, 0.0, 0.5 * (a + behind)),
            0.5 * (a + above),
            0.5 * (a + below),
        ]
        for nb in range(6):
            for c in range(COMPS):
                w = weight(c, nb // 2)
                face_ref[k, nb, c * NL : (c + 1) * NL, :] = faces[nb] * w if w != 1.0 else faces[nb]
    def invert(j, carry):
        for k in range(KM - 1):
            inv_ref[k, pair_ref[k, j]] = j
        return carry

    lax.fori_loop(0, total_modes, invert, 0)
    flat = spec_ref[...].reshape(NL * 2 * fields, LANES)
    term = jnp.dot(flat, sine_ref[...], precision=HIGHEST, preferred_element_type=jnp.float32)
    term = term.reshape(NL, 2, fields, LANES)
    for part in range(2):
        dst = field_ref if part == 0 else ends_ref
        for base in range(0, fields, 8):
            y = [term[m, part, base : base + 8, :] for m in range(NL)]
            for l in range(NL // 2):
                even = y[0] * float(COS[l, 0])
                odd = y[1] * float(COS[l, 1])
                for m in range(2, NL, 2):
                    even = even + y[m] * float(COS[l, m])
                    odd = odd + y[m + 1] * float(COS[l, m + 1])
                dst[pl.ds(base * NL + l, 8, stride=NL), :] = even + odd
                dst[pl.ds(base * NL + NL - 1 - l, 8, stride=NL), :] = even - odd
    span = COMPS * NL
    low, first, last = lane_masks(span)

    def stencils(j, carry):
        at = pl.ds(pl.multiple_of(j * span, 8), span)
        mid = field_ref[at, :]
        right, left = neighbours(mid, ends_ref[at, :], low)
        diffs = [
            mid - right,
            mid - left,
            mid - pltpu.roll(mid, span - 1, 0),
            mid - pltpu.roll(mid, 1, 0),
            mid - jnp.where(last, 0.0, pltpu.roll(mid, LANES - 1, 1)),
            mid - jnp.where(first, 0.0, pltpu.roll(mid, 1, 1)),
        ]
        for k in range(KM):
            acc = face_ref[k, 0] * diffs[0]
            for nb in range(1, 6):
                acc = acc + face_ref[k, nb] * diffs[nb]
            term_ref[k, j] = acc
        return carry

    lax.fori_loop(0, modes, stencils, 0)
    row_start = row_ref[0]

    def mixed(i, acc):
        for k in range(KM - 1):
            for way in range(2):
                partner = pair_ref[k, i] if way == 0 else inv_ref[k, i]
                coef = 0.5 * (coup_ref[k, i] if way == 0 else coup_ref[k, partner])
                local = partner - row_start
                inside = jnp.logical_and(local >= 0, local < modes)
                coef = jnp.where(inside, coef, 0.0)
                local = jnp.clip(local, 0, modes - 1)
                part = coef * term_ref[k + 1, local]
                acc = part if acc is None else acc + part
        return acc

    other_start = total_modes - modes - row_start

    def mix(i, carry):
        at = pl.ds(pl.multiple_of(i * span, 8), span)
        cross_ref[at, :] = mixed(other_start + i, None)
        own_ref[at, :] = mixed(row_start + i, term_ref[0, i])
        return carry

    lax.fori_loop(0, modes, mix, 0)
    pad = fields * NL - modes * span
    if pad:
        zero = jnp.zeros((pad, LANES), jnp.float32)
        cross_ref[modes * span :, :] = zero
        own_ref[modes * span :, :] = zero
        field_ref[modes * span :, :] = zero


def sums_kernel(rows, b_ref, u_ref, v_ref, z_ref, own_ref, recv_ref, image_ref, part_ref):
    q = own_ref[...] + recv_ref[...]
    image_ref[...] = q
    b, u, v, z = b_ref[...], u_ref[...], v_ref[...], z_ref[...]

    def fold(x):
        x = jnp.sum(x.reshape(rows // 8, 8, LANES), axis=0)
        return jnp.sum(x, axis=0, keepdims=True)

    sums = [fold(b * u), fold(u * v), fold(v * z), fold(b * z), fold(z * q)]
    sums += [jnp.zeros((3, LANES), jnp.float32)]
    part = jnp.concatenate(sums, axis=0)
    for i in range(part_ref.shape[0]):
        part_ref[i] = part


def final_kernel(parts_ref, b_ref, u_ref, v_ref, z_ref, q_ref, x_ref, r_ref):
    total = jnp.sum(jnp.sum(parts_ref[...], axis=0), axis=1, keepdims=True)
    bu, uv, vz, bz, zq = (total[i : i + 1, :] for i in range(5))
    a0 = bu / uv
    t = vz / uv
    c1 = (bz - a0 * vz) / (zq - t * vz)
    c0 = a0 - c1 * t
    x_ref[...] = c0 * u_ref[...] + c1 * z_ref[...]
    r_ref[...] = b_ref[...] - c0 * v_ref[...] - c1 * q_ref[...]


def on_device(right_side, stiffness, pairing, coupling):
    modes, comps, local_circ, num_cells = right_side.shape
    circ = lax.axis_size("circ")
    mode_blocks = lax.axis_size("mode")
    n_circ = local_circ * circ
    fields = -(-(modes * comps) // 8) * 8
    rows = fields * NL
    pad_fields = fields - modes * comps
    f32 = jnp.float32

    def struct(*shape):
        return jax.ShapeDtypeStruct(shape, f32)

    sine = jnp.asarray(sine_pair())
    b = right_side.reshape(modes * comps, local_circ, NL, NT)
    b = jnp.swapaxes(b, 1, 2).reshape(modes * comps * NL, LANES)
    b = jnp.pad(b, ((0, pad_fields * NL), (0, 0)))
    stiff = jnp.swapaxes(stiffness.reshape(KM, local_circ, NL, NT), 1, 2).reshape(KM, NL, LANES)
    ahead = [(i, (i + 1) % circ) for i in range(circ)]
    back = [((i + 1) % circ, i) for i in range(circ)]
    stiff_l = lax.ppermute(stiff, "circ", ahead)
    stiff_r = lax.ppermute(stiff, "circ", back)
    row_start = (lax.axis_index("mode") * modes).astype(jnp.int32).reshape(1)
    me = lax.axis_index("circ").astype(jnp.int32)

    split = circ // NL
    if split == 1:
        table = lax.dynamic_index_in_dim(jnp.asarray(circulant_table(n_circ)), me, 0, keepdims=False)

        def round_trip(spec):
            spec = lax.all_to_all(spec, "circ", split_axis=0, concat_axis=0)
            spec = pl.pallas_call(
                lambda *refs: circ_kernel(fields, circ, *refs),
                out_shape=struct(circ, 2, fields, LANES),
                in_specs=[whole()] * 2,
                out_specs=whole(),
                compiler_params=params(),
            )(spec, table)
            return lax.all_to_all(spec, "circ", split_axis=0, concat_axis=0)

    else:
        span = NT // split
        htab = jnp.asarray(hartley_np(n_circ), f32)
        denom = jnp.asarray(denominator_np(n_circ), f32).reshape(comps, n_circ, NL, split, span)
        denom = denom.transpose(2, 3, 0, 1, 4).reshape(circ, comps, n_circ, span)
        denom = lax.dynamic_index_in_dim(denom, me, 0, keepdims=False)

        def round_trip(spec):
            spec = spec.reshape(NL, fields, local_circ, split, span).transpose(0, 3, 1, 2, 4)
            spec = spec.reshape(circ, fields, local_circ, span)
            spec = lax.all_to_all(spec, "circ", split_axis=0, concat_axis=0)
            spec = spec[:, : modes * comps]
            spec = jnp.einsum("cfes,cek->fks", spec, htab.reshape(circ, local_circ, n_circ), precision=HIGHEST)
            spec = spec.reshape(modes, comps, n_circ, span) / denom[None]
            spec = jnp.einsum("pcks,kn->npcs", spec, htab, precision=HIGHEST)
            spec = spec.reshape(n_circ, modes * comps, span)
            spec = jnp.pad(spec, ((0, 0), (0, pad_fields), (0, 0)))
            own = spec.reshape(circ, local_circ, fields, span)
            after = jnp.roll(own[:, 0], -1, axis=0)
            before = jnp.roll(own[:, -1], 1, axis=0)
            spec = jnp.stack([own[:, 0], own[:, 1], after, before], axis=1)
            spec = lax.all_to_all(spec, "circ", split_axis=0, concat_axis=0)
            spec = spec.reshape(NL, split, 2, 2, fields, span).transpose(0, 2, 4, 3, 1, 5)
            return spec.reshape(NL, 2, fields, LANES)

    def operate(spec):
        return pl.pallas_call(
            lambda *refs: operator_kernel(modes, fields, *refs),
            out_shape=[struct(rows, LANES)] * 3,
            in_specs=[smem()] * 3 + [whole()] * 5,
            out_specs=[whole()] * 3,
            scratch_shapes=[
                pltpu.VMEM((8, LANES), f32),
                pltpu.VMEM((rows, LANES), f32),
                pltpu.VMEM((KM, 6, COMPS * NL, LANES), f32),
                pltpu.VMEM((KM, modes, COMPS * NL, LANES), f32),
                pltpu.SMEM((KM - 1, modes * mode_blocks), jnp.int32),
            ],
            compiler_params=params(),
        )(row_start, pairing, coupling, spec, sine, stiff, stiff_l, stiff_r)

    swap = [(0, 1), (1, 0)]

    spec = pl.pallas_call(
        lambda *refs: first_kernel(fields, *refs),
        out_shape=struct(NL, fields, LANES),
        in_specs=[whole()] * 2,
        out_specs=whole(),
        compiler_params=params(),
    )(b, sine)
    u, own, cross = operate(round_trip(spec))
    recv = lax.ppermute(cross, "mode", swap)
    spec, v = pl.pallas_call(
        lambda *refs: next_kernel(fields, *refs),
        out_shape=[struct(NL, fields, LANES), struct(rows, LANES)],
        in_specs=[whole()] * 4,
        out_specs=[whole()] * 2,
        scratch_shapes=[pltpu.VMEM((rows, LANES), f32)],
        compiler_params=params(),
    )(b, own, recv, sine)
    z, own, cross = operate(round_trip(spec))
    recv = lax.ppermute(cross, "mode", swap)
    devices = circ * mode_blocks
    q, part = pl.pallas_call(
        lambda *refs: sums_kernel(rows, *refs),
        out_shape=[struct(rows, LANES), struct(devices, 8, LANES)],
        in_specs=[whole()] * 6,
        out_specs=[whole()] * 2,
        compiler_params=params(),
    )(b, u, v, z, own, recv)
    parts = lax.all_to_all(part, ("circ", "mode"), split_axis=0, concat_axis=0)
    x, r = pl.pallas_call(
        final_kernel,
        out_shape=[struct(rows, LANES)] * 2,
        in_specs=[whole()] * 6,
        out_specs=[whole()] * 2,
        compiler_params=params(),
    )(parts, b, u, v, z, q)

    def give(values):
        values = values[: modes * comps * NL].reshape(modes * comps, NL, local_circ, NT)
        return jnp.swapaxes(values, 1, 2).reshape(right_side.shape)

    return give(x), give(r)


def solution(mesh):
    placed = (P("mode", None, "circ", None), P(None, "circ", None), P(), P())
    return jax.shard_map(
        on_device,
        mesh=mesh,
        in_specs=placed,
        out_specs=(P("mode", None, "circ", None), P("mode", None, "circ", None)),
        check_vma=False,
    )
```

```python
import math

import jax
import jax.numpy as jnp
import numpy as np
from jax import lax
from jax.experimental import pallas as pl
from jax.experimental.pallas import tpu as pltpu
from jax.sharding import PartitionSpec as P

KM = 4
NL = 16
NT = 64
COMPS = 3
LANES = 2 * NT
HIGHEST = lax.Precision.HIGHEST

SHIFT = 2.0 / 3.0


def weight(comp, direction):
    return 2.0 if comp == direction else 1.0


def cosine_np():
    l = np.arange(NL)
    return np.cos(math.pi * l[None, :] * (2 * l[:, None] + 1) / (2 * NL))


def sine_np():
    t = np.arange(NT) + 1
    return np.sin(math.pi * t[:, None] * t[None, :] / (NT + 1))


def hartley_np(size):
    n = np.arange(size)
    angle = 2.0 * math.pi / size * (n[:, None] * n[None, :] % size)
    return np.cos(angle) + np.sin(angle)


def denominator_np(n_circ):
    lam_c = 2.0 - 2.0 * np.cos(2.0 * math.pi / n_circ * np.arange(n_circ))[:, None, None]
    lam_l = 2.0 - 2.0 * np.cos(math.pi / NL * np.arange(NL))[None, :, None]
    lam_t = 2.0 - 2.0 * np.cos(math.pi / (NT + 1) * (np.arange(NT) + 1))[None, None, :]
    norm = np.where(np.arange(NL) == 0, 1.0 * NL, 0.5 * NL)[None, :, None]
    rows = [weight(c, 0) * lam_c + weight(c, 1) * lam_l + weight(c, 2) * lam_t for c in range(COMPS)]
    return np.stack(rows) * (n_circ * norm * (0.5 * (NT + 1)))


COS = cosine_np()


def sine_pair():
    both = np.zeros((LANES, LANES))
    both[:NT, :NT] = sine_np()
    both[NT:, NT:] = sine_np()
    return both.astype(np.float32)


def circulant_table(n_circ):
    half = n_circ // 2
    quarter = half // 2
    freq = np.arange(n_circ)
    inverse = 1.0 / denominator_np(n_circ)
    turn = np.cos(2.0 * math.pi / n_circ * (freq[:, None] * freq[None, :] % n_circ))
    g = np.einsum("dk,ckms->dcms", turn, inverse)
    same = np.stack([np.concatenate([g[2 * d], g[2 * d]], -1) for d in range(half)])
    cross = np.stack(
        [np.concatenate([g[(2 * d - 1) % n_circ], g[(2 * d + 1) % n_circ]], -1) for d in range(half)]
    )
    parts = []
    for full in (same, cross):
        parts.append(0.5 * (full[:quarter] + full[quarter:]))
        parts.append(0.5 * (full[:quarter] - full[quarter:]))
    table = np.stack(parts)
    return np.transpose(table, (3, 0, 1, 2, 4)).astype(np.float32)


def whole():
    return pl.BlockSpec(memory_space=pltpu.VMEM)


def smem():
    return pl.BlockSpec(memory_space=pltpu.SMEM)


def params():
    return pltpu.CompilerParams(vmem_limit_bytes=32 * 1024 * 1024)


def forward_rows(load, sine_ref, out_ref, fields):
    for base in range(0, fields, 8):
        plus, minus = [], []
        for l in range(NL // 2):
            a, b = load(l, base), load(NL - 1 - l, base)
            plus.append(a + b)
            minus.append(a - b)
        for m in range(NL):
            src = plus if m % 2 == 0 else minus
            acc = src[0] * float(COS[0, m])
            for l in range(1, NL // 2):
                acc = acc + src[l] * float(COS[l, m])
            out_ref[m, base : base + 8, :] = acc
    flat = out_ref[...].reshape(NL * fields, LANES)
    done = jnp.dot(flat, sine_ref[...], precision=HIGHEST, preferred_element_type=jnp.float32)
    out_ref[...] = done.reshape(NL, fields, LANES)


def deal(me_ref, all_ref, out_refs):
    if len(out_refs) == 1:
        out_refs[0][...] = all_ref[...]
    else:
        for d, ref in enumerate(out_refs):
            ref[...] = all_ref[me_ref[0] ^ d]


def collect(me_ref, in_refs, all_ref):
    if len(in_refs) == 1:
        all_ref[...] = in_refs[0][...]
    else:
        for d, ref in enumerate(in_refs):
            all_ref[me_ref[0] ^ d] = ref[...]


def first_kernel(fields, me_ref, b_ref, sine_ref, *refs):
    *out_refs, all_ref = refs
    forward_rows(lambda l, base: b_ref[pl.ds(base * NL + l, 8, stride=NL), :], sine_ref, all_ref, fields)
    deal(me_ref, all_ref, out_refs)


def next_kernel(fields, me_ref, b_ref, own_ref, recv_ref, sine_ref, *refs):
    *out_refs, image_ref, work_ref, all_ref = refs
    image = own_ref[...] + recv_ref[...]
    image_ref[...] = image
    work_ref[...] = b_ref[...] - SHIFT * image
    forward_rows(lambda l, base: work_ref[pl.ds(base * NL + l, 8, stride=NL), :], sine_ref, all_ref, fields)
    deal(me_ref, all_ref, out_refs)


def circ_kernel(fields, half, me_ref, table_ref, *refs):
    in_refs, out_refs = refs[:half], refs[half : 2 * half]
    x_ref, out_ref = refs[2 * half :]
    collect(me_ref, in_refs, x_ref)
    quarter = half // 2
    comp_row = lax.broadcasted_iota(jnp.int32, (8, LANES), 0)
    low = lax.broadcasted_iota(jnp.int32, (8, LANES), 1) < NT
    for base in range(0, fields, 8):
        comp = (comp_row + base) % COMPS

        def spread(part, d):
            rows = table_ref[part, d]
            return jnp.where(comp == 0, rows[0:1], jnp.where(comp == 1, rows[1:2], rows[2:3]))

        coef = [[spread(part, d) for d in range(quarter)] for part in range(4)]
        plus, minus, plus_x, minus_x = [], [], [], []
        for c in range(quarter):
            a = x_ref[c, base : base + 8, :]
            b = x_ref[c + quarter, base : base + 8, :]
            plus.append(a + b)
            minus.append(a - b)
            plus_x.append(pltpu.roll(a + b, NT, 1))
            minus_x.append(pltpu.roll(a - b, NT, 1))
        outs = [None] * half
        for c in range(quarter):
            even = odd = None
            for e in range(quarter):
                d = (c - e) % quarter
                term = coef[0][d] * plus[e] + coef[2][d] * plus_x[e]
                even = term if even is None else even + term
                term = coef[1][d] * minus[e] + coef[3][d] * minus_x[e]
                if c < e:
                    term = -term
                odd = term if odd is None else odd + term
            outs[c] = even + odd
            outs[c + quarter] = even - odd
        for c in range(half):
            out_ref[c, 0, base : base + 8, :] = outs[c]
            out_ref[c, 1, base : base + 8, :] = jnp.where(low, outs[(c + 1) % half], outs[c - 1])
    deal(me_ref, out_ref, out_refs)


def lane_masks(rows):
    lane = lax.broadcasted_iota(jnp.int32, (rows, LANES), 1)
    return lane < NT, lane % NT == 0, lane % NT == NT - 1


def neighbours(mid, ends, low):
    right = pltpu.roll(jnp.where(low, ends, mid), NT, 1)
    left = pltpu.roll(jnp.where(low, mid, ends), NT, 1)
    return right, left


def operator_kernel(
    modes, fields, me_ref, row_ref, pair_ref, coup_ref, sine_ref, stiff_ref, stiff_l_ref, stiff_r_ref, *refs
):
    *spec_refs, field_ref, own_ref, cross_ref, spec_ref, ends_ref, face_ref, term_ref, inv_ref = refs
    collect(me_ref, spec_refs, spec_ref)
    total_modes = pair_ref.shape[1]
    low, first, last = lane_masks(NL)
    row = lax.broadcasted_iota(jnp.int32, (NL, LANES), 0)
    for k in range(KM):
        a = stiff_ref[k]
        ends = jnp.where(low, stiff_r_ref[k], stiff_l_ref[k])
        right, left = neighbours(a, ends, low)
        above = jnp.where(last, a, pltpu.roll(a, LANES - 1, 1))
        below = jnp.where(first, a, pltpu.roll(a, 1, 1))
        ahead = pltpu.roll(a, NL - 1, 0)
        behind = pltpu.roll(a, 1, 0)
        faces = [
            0.5 * (a + right),
            0.5 * (a + left),
            jnp.where(row == NL - 1, 0.0, 0.5 * (a + ahead)),
            jnp.where(row == 0, 0.0, 0.5 * (a + behind)),
            0.5 * (a + above),
            0.5 * (a + below),
        ]
        for nb in range(6):
            for c in range(COMPS):
                w = weight(c, nb // 2)
                face_ref[k, nb, c * NL : (c + 1) * NL, :] = faces[nb] * w if w != 1.0 else faces[nb]
    def invert(j, carry):
        for k in range(KM - 1):
            inv_ref[k, pair_ref[k, j]] = j
        return carry

    lax.fori_loop(0, total_modes, invert, 0)
    flat = spec_ref[...].reshape(NL * 2 * fields, LANES)
    term = jnp.dot(flat, sine_ref[...], precision=HIGHEST, preferred_element_type=jnp.float32)
    term = term.reshape(NL, 2, fields, LANES)
    for part in range(2):
        dst = field_ref if part == 0 else ends_ref
        for base in range(0, fields, 8):
            y = [term[m, part, base : base + 8, :] for m in range(NL)]
            for l in range(NL // 2):
                even = y[0] * float(COS[l, 0])
                odd = y[1] * float(COS[l, 1])
                for m in range(2, NL, 2):
                    even = even + y[m] * float(COS[l, m])
                    odd = odd + y[m + 1] * float(COS[l, m + 1])
                dst[pl.ds(base * NL + l, 8, stride=NL), :] = even + odd
                dst[pl.ds(base * NL + NL - 1 - l, 8, stride=NL), :] = even - odd
    span = COMPS * NL
    low, first, last = lane_masks(span)

    def stencils(j, carry):
        at = pl.ds(pl.multiple_of(j * span, 8), span)
        mid = field_ref[at, :]
        right, left = neighbours(mid, ends_ref[at, :], low)
        diffs = [
            mid - right,
            mid - left,
            mid - pltpu.roll(mid, span - 1, 0),
            mid - pltpu.roll(mid, 1, 0),
            mid - jnp.where(last, 0.0, pltpu.roll(mid, LANES - 1, 1)),
            mid - jnp.where(first, 0.0, pltpu.roll(mid, 1, 1)),
        ]
        for k in range(KM):
            acc = face_ref[k, 0] * diffs[0]
            for nb in range(1, 6):
                acc = acc + face_ref[k, nb] * diffs[nb]
            term_ref[k, j] = acc
        return carry

    lax.fori_loop(0, modes, stencils, 0)
    row_start = row_ref[0]

    def mixed(i, acc):
        for k in range(KM - 1):
            for way in range(2):
                partner = pair_ref[k, i] if way == 0 else inv_ref[k, i]
                coef = 0.5 * (coup_ref[k, i] if way == 0 else coup_ref[k, partner])
                local = partner - row_start
                inside = jnp.logical_and(local >= 0, local < modes)
                coef = jnp.where(inside, coef, 0.0)
                local = jnp.clip(local, 0, modes - 1)
                part = coef * term_ref[k + 1, local]
                acc = part if acc is None else acc + part
        return acc

    other_start = total_modes - modes - row_start

    def mix(i, carry):
        at = pl.ds(pl.multiple_of(i * span, 8), span)
        cross_ref[at, :] = mixed(other_start + i, None)
        own_ref[at, :] = mixed(row_start + i, term_ref[0, i])
        return carry

    lax.fori_loop(0, modes, mix, 0)
    pad = fields * NL - modes * span
    if pad:
        zero = jnp.zeros((pad, LANES), jnp.float32)
        cross_ref[modes * span :, :] = zero
        own_ref[modes * span :, :] = zero
        field_ref[modes * span :, :] = zero


def sums_kernel(rows, b_ref, u_ref, v_ref, z_ref, own_ref, recv_ref, image_ref, part_ref):
    q = own_ref[...] + recv_ref[...]
    image_ref[...] = q
    b, u, v, z = b_ref[...], u_ref[...], v_ref[...], z_ref[...]

    def fold(x):
        x = jnp.sum(x.reshape(rows // 8, 8, LANES), axis=0)
        return jnp.sum(x, axis=0, keepdims=True)

    sums = [fold(b * u), fold(u * v), fold(v * z), fold(b * z), fold(z * q)]
    sums += [jnp.zeros((3, LANES), jnp.float32)]
    part = jnp.concatenate(sums, axis=0)
    for i in range(part_ref.shape[0]):
        part_ref[i] = part


def final_kernel(parts_ref, b_ref, u_ref, v_ref, z_ref, q_ref, x_ref, r_ref):
    total = jnp.sum(jnp.sum(parts_ref[...], axis=0), axis=1, keepdims=True)
    bu, uv, vz, bz, zq = (total[i : i + 1, :] for i in range(5))
    a0 = bu / uv
    t = vz / uv
    c1 = (bz - a0 * vz) / (zq - t * vz)
    c0 = a0 - c1 * t
    x_ref[...] = c0 * u_ref[...] + c1 * z_ref[...]
    r_ref[...] = b_ref[...] - c0 * v_ref[...] - c1 * q_ref[...]


def on_device(right_side, stiffness, pairing, coupling):
    modes, comps, local_circ, num_cells = right_side.shape
    circ = lax.axis_size("circ")
    mode_blocks = lax.axis_size("mode")
    n_circ = local_circ * circ
    fields = -(-(modes * comps) // 8) * 8
    rows = fields * NL
    pad_fields = fields - modes * comps
    f32 = jnp.float32

    def struct(*shape):
        return jax.ShapeDtypeStruct(shape, f32)

    sine = jnp.asarray(sine_pair())
    b = right_side.reshape(modes * comps, local_circ, NL, NT)
    b = jnp.swapaxes(b, 1, 2).reshape(modes * comps * NL, LANES)
    b = jnp.pad(b, ((0, pad_fields * NL), (0, 0)))
    stiff = jnp.swapaxes(stiffness.reshape(KM, local_circ, NL, NT), 1, 2).reshape(KM, NL, LANES)
    ahead = [(i, (i + 1) % circ) for i in range(circ)]
    back = [((i + 1) % circ, i) for i in range(circ)]
    stiff_l = lax.ppermute(stiff, "circ", ahead)
    stiff_r = lax.ppermute(stiff, "circ", back)
    row_start = (lax.axis_index("mode") * modes).astype(jnp.int32).reshape(1)
    me = lax.axis_index("circ").astype(jnp.int32).reshape(1)

    split = circ // NL
    pieces = circ if split == 1 else 1
    chunks = [struct(fields, LANES)] * circ if split == 1 else [struct(NL, fields, LANES)]
    if split == 1:
        table = lax.dynamic_index_in_dim(jnp.asarray(circulant_table(n_circ)), me[0], 0, keepdims=False)

        def exchange(parts):
            return [parts[0]] + [
                lax.ppermute(parts[d], "circ", [(i, i ^ d) for i in range(circ)]) for d in range(1, circ)
            ]

        def round_trip(parts):
            parts = pl.pallas_call(
                lambda *refs: circ_kernel(fields, circ, *refs),
                out_shape=[struct(2, fields, LANES)] * circ,
                in_specs=[smem()] + [whole()] * (1 + circ),
                out_specs=[whole()] * circ,
                scratch_shapes=[
                    pltpu.VMEM((circ, fields, LANES), f32),
                    pltpu.VMEM((circ, 2, fields, LANES), f32),
                ],
                compiler_params=params(),
            )(me, table, *exchange(parts))
            return exchange(parts)

    else:
        span = NT // split
        htab = jnp.asarray(hartley_np(n_circ), f32)
        denom = jnp.asarray(denominator_np(n_circ), f32).reshape(comps, n_circ, NL, split, span)
        denom = denom.transpose(2, 3, 0, 1, 4).reshape(circ, comps, n_circ, span)
        denom = lax.dynamic_index_in_dim(denom, me[0], 0, keepdims=False)

        def round_trip(parts):
            spec = parts[0].reshape(NL, fields, local_circ, split, span).transpose(0, 3, 1, 2, 4)
            spec = spec.reshape(circ, fields, local_circ, span)
            spec = lax.all_to_all(spec, "circ", split_axis=0, concat_axis=0)
            spec = spec[:, : modes * comps]
            spec = jnp.einsum("cfes,cek->fks", spec, htab.reshape(circ, local_circ, n_circ), precision=HIGHEST)
            spec = spec.reshape(modes, comps, n_circ, span) / denom[None]
            spec = jnp.einsum("pcks,kn->npcs", spec, htab, precision=HIGHEST)
            spec = spec.reshape(n_circ, modes * comps, span)
            spec = jnp.pad(spec, ((0, 0), (0, pad_fields), (0, 0)))
            own = spec.reshape(circ, local_circ, fields, span)
            after = jnp.roll(own[:, 0], -1, axis=0)
            before = jnp.roll(own[:, -1], 1, axis=0)
            spec = jnp.stack([own[:, 0], own[:, 1], after, before], axis=1)
            spec = lax.all_to_all(spec, "circ", split_axis=0, concat_axis=0)
            spec = spec.reshape(NL, split, 2, 2, fields, span).transpose(0, 2, 4, 3, 1, 5)
            return [spec.reshape(NL, 2, fields, LANES)]

    def operate(parts):
        return pl.pallas_call(
            lambda *refs: operator_kernel(modes, fields, *refs),
            out_shape=[struct(rows, LANES)] * 3,
            in_specs=[smem()] * 4 + [whole()] * (4 + pieces),
            out_specs=[whole()] * 3,
            scratch_shapes=[
                pltpu.VMEM((NL, 2, fields, LANES), f32),
                pltpu.VMEM((rows, LANES), f32),
                pltpu.VMEM((KM, 6, COMPS * NL, LANES), f32),
                pltpu.VMEM((KM, modes, COMPS * NL, LANES), f32),
                pltpu.SMEM((KM - 1, modes * mode_blocks), jnp.int32),
            ],
            compiler_params=params(),
        )(me, row_start, pairing, coupling, sine, stiff, stiff_l, stiff_r, *parts)

    swap = [(0, 1), (1, 0)]

    parts = pl.pallas_call(
        lambda *refs: first_kernel(fields, *refs),
        out_shape=chunks,
        in_specs=[smem()] + [whole()] * 2,
        out_specs=[whole()] * pieces,
        scratch_shapes=[pltpu.VMEM((NL, fields, LANES), f32)],
        compiler_params=params(),
    )(me, b, sine)
    u, own, cross = operate(round_trip(parts))
    recv = lax.ppermute(cross, "mode", swap)
    *parts, v = pl.pallas_call(
        lambda *refs: next_kernel(fields, *refs),
        out_shape=chunks + [struct(rows, LANES)],
        in_specs=[smem()] + [whole()] * 4,
        out_specs=[whole()] * (pieces + 1),
        scratch_shapes=[pltpu.VMEM((rows, LANES), f32), pltpu.VMEM((NL, fields, LANES), f32)],
        compiler_params=params(),
    )(me, b, own, recv, sine)
    z, own, cross = operate(round_trip(parts))
    recv = lax.ppermute(cross, "mode", swap)
    devices = circ * mode_blocks
    q, part = pl.pallas_call(
        lambda *refs: sums_kernel(rows, *refs),
        out_shape=[struct(rows, LANES), struct(devices, 8, LANES)],
        in_specs=[whole()] * 6,
        out_specs=[whole()] * 2,
        compiler_params=params(),
    )(b, u, v, z, own, recv)
    parts = lax.all_to_all(part, ("circ", "mode"), split_axis=0, concat_axis=0)
    x, r = pl.pallas_call(
        final_kernel,
        out_shape=[struct(rows, LANES)] * 2,
        in_specs=[whole()] * 6,
        out_specs=[whole()] * 2,
        compiler_params=params(),
    )(parts, b, u, v, z, q)

    def give(values):
        values = values[: modes * comps * NL].reshape(modes * comps, NL, local_circ, NT)
        return jnp.swapaxes(values, 1, 2).reshape(right_side.shape)

    return give(x), give(r)


def solution(mesh):
    placed = (P("mode", None, "circ", None), P(None, "circ", None), P(), P())
    return jax.shard_map(
        on_device,
        mesh=mesh,
        in_specs=placed,
        out_specs=(P("mode", None, "circ", None), P("mode", None, "circ", None)),
        check_vma=False,
    )
```

```python
import functools
import math

import jax
import jax.numpy as jnp
import numpy as np
from jax import lax
from jax.experimental import pallas as pl
from jax.experimental.pallas import tpu as pltpu
from jax.sharding import PartitionSpec as P

KM = 4
NL = 16
NT = 64
COMPS = 3
LANES = 2 * NT
HIGHEST = lax.Precision.HIGHEST

SHIFT = 2.0 / 3.0


def weight(comp, direction):
    return 2.0 if comp == direction else 1.0


def cosine_np():
    l = np.arange(NL)
    return np.cos(math.pi * l[None, :] * (2 * l[:, None] + 1) / (2 * NL))


def sine_np():
    t = np.arange(NT) + 1
    return np.sin(math.pi * t[:, None] * t[None, :] / (NT + 1))


COS = cosine_np()


def sine_pair():
    both = np.zeros((LANES, LANES))
    both[:NT, :NT] = sine_np()
    both[NT:, NT:] = sine_np()
    return both.astype(np.float32)


def root_np():
    lam_l = 2.0 - 2.0 * np.cos(math.pi / NL * np.arange(NL))[:, None]
    lam_t = 2.0 - 2.0 * np.cos(math.pi / (NT + 1) * (np.arange(NT) + 1))[None, :]
    norm = np.where(np.arange(NL) == 0, 1.0 * NL, 0.5 * NL)[:, None] * (0.5 * (NT + 1))
    roots, scales = [], []
    for c in range(COMPS):
        w = weight(c, 0)
        half = 1.0 + (weight(c, 1) * lam_l + weight(c, 2) * lam_t) / (2.0 * w)
        big = half + np.sqrt(half * half - 1.0)
        roots.append(1.0 / big)
        scales.append(1.0 / (w * (big - 1.0 / big) * norm))
    return np.stack(roots), np.stack(scales)


def by_core(table):
    table = np.moveaxis(table, -2, -3)
    lead = table.shape[:-3]
    table = table.reshape(lead + (2, NL // 2) + table.shape[-2:])
    return np.moveaxis(table, len(lead), 0).astype(np.float32)


def power_table(n_circ):
    root, _ = root_np()
    powers = root[None] ** np.arange(n_circ - 6)[:, None, None, None]
    return by_core(np.concatenate([powers, powers], -1))


def cell_table(n_circ):
    root, scale = root_np()
    scale = scale / (1.0 - root**n_circ)

    def kernel(d):
        return scale * (root ** abs(d) + root ** (n_circ - abs(d)))

    out = []
    for low, high in ((0, 1), (2, 3), (4, -1)):
        for first, second in ((0, 1), (1, 0), (2, 3), (3, 2)):
            out.append(np.concatenate([kernel(low - first), kernel(high - second)], -1))
        out.append(np.concatenate([scale * root ** (3.0 - low), scale * root ** float(high)], -1))
        out.append(np.concatenate([scale * root ** float(low), scale * root ** (3.0 - high)], -1))
    return by_core(np.stack(out))


def whole():
    return pl.BlockSpec(memory_space=pltpu.VMEM)


def smem():
    return pl.BlockSpec(memory_space=pltpu.SMEM)


def params():
    return pltpu.CompilerParams(vmem_limit_bytes=32 * 1024 * 1024)


def forward_rows(load, sine_ref, out_ref, fields):
    for base in range(0, fields, 8):
        plus, minus = [], []
        for l in range(NL // 2):
            a, b = load(l, base), load(NL - 1 - l, base)
            plus.append(a + b)
            minus.append(a - b)
        for m in range(NL):
            src = plus if m % 2 == 0 else minus
            acc = src[0] * float(COS[0, m])
            for l in range(1, NL // 2):
                acc = acc + src[l] * float(COS[l, m])
            out_ref[m, base : base + 8, :] = acc
    flat = out_ref[...].reshape(NL * fields, LANES)
    done = jnp.dot(flat, sine_ref[...], precision=HIGHEST, preferred_element_type=jnp.float32)
    out_ref[...] = done.reshape(NL, fields, LANES)


def deal(me_ref, all_ref, keep_ref, send_ref):
    core = me_ref[0] & 1
    half = NL // 2
    keep_ref[...] = all_ref[pl.ds(core * half, half)]
    send_ref[...] = all_ref[pl.ds((1 - core) * half, half)]


def first_kernel(fields, me_ref, b_ref, sine_ref, keep_ref, send_ref, all_ref):
    forward_rows(lambda l, base: b_ref[pl.ds(base * NL + l, 8, stride=NL), :], sine_ref, all_ref, fields)
    deal(me_ref, all_ref, keep_ref, send_ref)


def next_kernel(fields, me_ref, b_ref, own_ref, recv_ref, sine_ref, keep_ref, send_ref, image_ref, work_ref, all_ref):
    image = own_ref[...] + recv_ref[...]
    image_ref[...] = image
    work_ref[...] = b_ref[...] - SHIFT * image
    forward_rows(lambda l, base: work_ref[pl.ds(base * NL + l, 8, stride=NL), :], sine_ref, all_ref, fields)
    deal(me_ref, all_ref, keep_ref, send_ref)


def swap_halves(x):
    return pltpu.roll(x, NT, 1)


def columns(fields):
    comp_row = lax.broadcasted_iota(jnp.int32, (8, LANES), 0)

    def run(body):
        def step(m, carry):
            for base in range(0, fields, 8):
                comp = (comp_row + base) % COMPS

                def spread(rows):
                    return jnp.where(comp == 0, rows[0:1], jnp.where(comp == 1, rows[1:2], rows[2:3]))

                body(m, slice(base, base + 8), spread)
            return carry

        lax.fori_loop(0, NL // 2, step, 0)

    return run


def four_cells(core, keep, recv):
    first = jnp.where(core == 0, keep, recv)
    second = jnp.where(core == 0, recv, keep)
    return first, swap_halves(first), second, swap_halves(second)


def low_lanes(rows):
    return lax.broadcasted_iota(jnp.int32, (rows, LANES), 1) < NT


def ends_kernel(fields, me_ref, keep_ref, recv_ref, power_ref, ends_ref):
    core = me_ref[0] & 1
    low = low_lanes(COMPS)

    def body(m, at, spread):
        cells = four_cells(core, keep_ref[m, at, :], recv_ref[m, at, :])
        acc = None
        for cell, (a, b) in zip(cells, ((0, 2), (1, 3), (2, 0), (3, 1))):
            term = spread(jnp.where(low, power_ref[core, a, m], power_ref[core, b, m])) * cell
            acc = term if acc is None else acc + term
        ends_ref[m, at, :] = acc

    columns(fields)(body)


def stage_kernel(fields, n_circ, stage, last, me_ref, *refs):
    own_ref, recv_ref, power_ref = refs[:3]
    sum_ref = None if stage == 0 else refs[3]
    outs = refs[3 if stage == 0 else 4 :]
    me = me_ref[0]
    core, chip = me & 1, me >> 1
    block = 4 << stage
    bit = (chip >> stage) & 1
    place = 4 * (chip & ((1 << stage) - 1))
    right = jnp.where(bit == 0, block - 3 - place, n_circ - 3 - place - block)
    left = jnp.where(bit == 0, n_circ - 2 * block + place + 1, place + 1)
    low = low_lanes(COMPS)

    def pair(m, a, b):
        return jnp.where(low, power_ref[core, a, m], power_ref[core, b, m])

    def body(m, at, spread):
        other = recv_ref[m, at, :]
        total = spread(pair(m, right, left)) * other
        outs[0][m, at, :] = total if sum_ref is None else total + sum_ref[m, at, :]
        if not last:
            near, far = bit * block, (1 - bit) * block
            joined = spread(pair(m, near, far)) * own_ref[m, at, :] + spread(pair(m, far, near)) * other
            outs[1][m, at, :] = joined

    columns(fields)(body)


def cells_kernel(fields, me_ref, keep_ref, recv_ref, sum_ref, cell_ref, mine_ref, send_ref):
    core = me_ref[0] & 1
    low = low_lanes(8)

    def body(m, at, spread):
        outside = sum_ref[m, at, :]
        terms = four_cells(core, keep_ref[m, at, :], recv_ref[m, at, :]) + (outside, swap_halves(outside))
        cells = []
        for group in range(3):
            acc = None
            for i, term in enumerate(terms):
                part = spread(cell_ref[core, 6 * group + i, m]) * term
                acc = part if acc is None else acc + part
            cells.append(acc)
        near0 = jnp.where(low, cells[1], cells[2])
        near1 = jnp.where(low, cells[2], cells[0])
        mine_ref[m, 0, at, :] = jnp.where(core == 0, cells[0], cells[1])
        mine_ref[m, 1, at, :] = jnp.where(core == 0, near0, near1)
        send_ref[m, 0, at, :] = jnp.where(core == 0, cells[1], cells[0])
        send_ref[m, 1, at, :] = jnp.where(core == 0, near1, near0)

    columns(fields)(body)


def lane_masks(rows):
    lane = lax.broadcasted_iota(jnp.int32, (rows, LANES), 1)
    return lane < NT, lane % NT == 0, lane % NT == NT - 1


def neighbours(mid, ends, low):
    right = pltpu.roll(jnp.where(low, ends, mid), NT, 1)
    left = pltpu.roll(jnp.where(low, mid, ends), NT, 1)
    return right, left


def operator_kernel(
    modes, fields, me_ref, row_ref, pair_ref, coup_ref, sine_ref, stiff_ref, stiff_l_ref, stiff_r_ref, *refs
):
    keep_ref, recv_ref, field_ref, own_ref, cross_ref, spec_ref, ends_ref, face_ref, term_ref, inv_ref = refs
    core = me_ref[0] & 1
    spec_ref[pl.ds(core * (NL // 2), NL // 2)] = keep_ref[...]
    spec_ref[pl.ds((1 - core) * (NL // 2), NL // 2)] = recv_ref[...]
    total_modes = pair_ref.shape[1]
    low, first, last = lane_masks(NL)
    row = lax.broadcasted_iota(jnp.int32, (NL, LANES), 0)
    for k in range(KM):
        a = stiff_ref[k]
        ends = jnp.where(low, stiff_r_ref[k], stiff_l_ref[k])
        right, left = neighbours(a, ends, low)
        above = jnp.where(last, a, pltpu.roll(a, LANES - 1, 1))
        below = jnp.where(first, a, pltpu.roll(a, 1, 1))
        ahead = pltpu.roll(a, NL - 1, 0)
        behind = pltpu.roll(a, 1, 0)
        faces = [
            0.5 * (a + right),
            0.5 * (a + left),
            jnp.where(row == NL - 1, 0.0, 0.5 * (a + ahead)),
            jnp.where(row == 0, 0.0, 0.5 * (a + behind)),
            0.5 * (a + above),
            0.5 * (a + below),
        ]
        for nb in range(6):
            for c in range(COMPS):
                w = weight(c, nb // 2)
                face_ref[k, nb, c * NL : (c + 1) * NL, :] = faces[nb] * w if w != 1.0 else faces[nb]
    def invert(j, carry):
        for k in range(KM - 1):
            inv_ref[k, pair_ref[k, j]] = j
        return carry

    lax.fori_loop(0, total_modes, invert, 0)
    flat = spec_ref[...].reshape(NL * 2 * fields, LANES)
    term = jnp.dot(flat, sine_ref[...], precision=HIGHEST, preferred_element_type=jnp.float32)
    term = term.reshape(NL, 2, fields, LANES)
    for part in range(2):
        dst = field_ref if part == 0 else ends_ref
        for base in range(0, fields, 8):
            y = [term[m, part, base : base + 8, :] for m in range(NL)]
            for l in range(NL // 2):
                even = y[0] * float(COS[l, 0])
                odd = y[1] * float(COS[l, 1])
                for m in range(2, NL, 2):
                    even = even + y[m] * float(COS[l, m])
                    odd = odd + y[m + 1] * float(COS[l, m + 1])
                dst[pl.ds(base * NL + l, 8, stride=NL), :] = even + odd
                dst[pl.ds(base * NL + NL - 1 - l, 8, stride=NL), :] = even - odd
    span = COMPS * NL
    low, first, last = lane_masks(span)

    def stencils(j, carry):
        at = pl.ds(pl.multiple_of(j * span, 8), span)
        mid = field_ref[at, :]
        right, left = neighbours(mid, ends_ref[at, :], low)
        diffs = [
            mid - right,
            mid - left,
            mid - pltpu.roll(mid, span - 1, 0),
            mid - pltpu.roll(mid, 1, 0),
            mid - jnp.where(last, 0.0, pltpu.roll(mid, LANES - 1, 1)),
            mid - jnp.where(first, 0.0, pltpu.roll(mid, 1, 1)),
        ]
        for k in range(KM):
            acc = face_ref[k, 0] * diffs[0]
            for nb in range(1, 6):
                acc = acc + face_ref[k, nb] * diffs[nb]
            term_ref[k, j] = acc
        return carry

    lax.fori_loop(0, modes, stencils, 0)
    row_start = row_ref[0]

    def mixed(i, acc):
        for k in range(KM - 1):
            for way in range(2):
                partner = pair_ref[k, i] if way == 0 else inv_ref[k, i]
                coef = 0.5 * (coup_ref[k, i] if way == 0 else coup_ref[k, partner])
                local = partner - row_start
                inside = jnp.logical_and(local >= 0, local < modes)
                coef = jnp.where(inside, coef, 0.0)
                local = jnp.clip(local, 0, modes - 1)
                part = coef * term_ref[k + 1, local]
                acc = part if acc is None else acc + part
        return acc

    other_start = total_modes - modes - row_start

    def mix(i, carry):
        at = pl.ds(pl.multiple_of(i * span, 8), span)
        cross_ref[at, :] = mixed(other_start + i, None)
        own_ref[at, :] = mixed(row_start + i, term_ref[0, i])
        return carry

    lax.fori_loop(0, modes, mix, 0)
    pad = fields * NL - modes * span
    if pad:
        zero = jnp.zeros((pad, LANES), jnp.float32)
        cross_ref[modes * span :, :] = zero
        own_ref[modes * span :, :] = zero
        field_ref[modes * span :, :] = zero


def sums_kernel(rows, b_ref, u_ref, v_ref, z_ref, own_ref, recv_ref, image_ref, part_ref):
    q = own_ref[...] + recv_ref[...]
    image_ref[...] = q
    b, u, v, z = b_ref[...], u_ref[...], v_ref[...], z_ref[...]

    def fold(x):
        x = jnp.sum(x.reshape(rows // 8, 8, LANES), axis=0)
        return jnp.sum(x, axis=0, keepdims=True)

    sums = [fold(b * u), fold(u * v), fold(v * z), fold(b * z), fold(z * q)]
    sums += [jnp.zeros((3, LANES), jnp.float32)]
    part = jnp.concatenate(sums, axis=0)
    for i in range(part_ref.shape[0]):
        part_ref[i] = part


def final_kernel(parts_ref, b_ref, u_ref, v_ref, z_ref, q_ref, x_ref, r_ref):
    total = jnp.sum(jnp.sum(parts_ref[...], axis=0), axis=1, keepdims=True)
    bu, uv, vz, bz, zq = (total[i : i + 1, :] for i in range(5))
    a0 = bu / uv
    t = vz / uv
    c1 = (bz - a0 * vz) / (zq - t * vz)
    c0 = a0 - c1 * t
    x_ref[...] = c0 * u_ref[...] + c1 * z_ref[...]
    r_ref[...] = b_ref[...] - c0 * v_ref[...] - c1 * q_ref[...]


def on_device(right_side, stiffness, pairing, coupling):
    modes, comps, local_circ, num_cells = right_side.shape
    circ = lax.axis_size("circ")
    mode_blocks = lax.axis_size("mode")
    n_circ = local_circ * circ
    fields = -(-(modes * comps) // 8) * 8
    rows = fields * NL
    pad_fields = fields - modes * comps
    f32 = jnp.float32

    def struct(*shape):
        return jax.ShapeDtypeStruct(shape, f32)

    sine = jnp.asarray(sine_pair())
    b = right_side.reshape(modes * comps, local_circ, NL, NT)
    b = jnp.swapaxes(b, 1, 2).reshape(modes * comps * NL, LANES)
    b = jnp.pad(b, ((0, pad_fields * NL), (0, 0)))
    stiff = jnp.swapaxes(stiffness.reshape(KM, local_circ, NL, NT), 1, 2).reshape(KM, NL, LANES)
    ahead = [(i, (i + 1) % circ) for i in range(circ)]
    back = [((i + 1) % circ, i) for i in range(circ)]
    stiff_l = lax.ppermute(stiff, "circ", ahead)
    stiff_r = lax.ppermute(stiff, "circ", back)
    row_start = (lax.axis_index("mode") * modes).astype(jnp.int32).reshape(1)
    me = lax.axis_index("circ").astype(jnp.int32).reshape(1)

    half = struct(NL // 2, fields, LANES)
    pairs = struct(NL // 2, 2, fields, LANES)
    power = jnp.asarray(power_table(n_circ))
    cell = jnp.asarray(cell_table(n_circ))

    def call(kernel, out_shape, *args, scratch_shapes=()):
        single = not isinstance(out_shape, list)
        return pl.pallas_call(
            kernel,
            out_shape=out_shape,
            in_specs=[smem()] + [whole()] * (len(args) - 1),
            out_specs=whole() if single else [whole()] * len(out_shape),
            scratch_shapes=scratch_shapes,
            compiler_params=params(),
        )(*args)

    def partner(values, d):
        return lax.ppermute(values, "circ", [(i, i ^ d) for i in range(circ)])

    def round_trip(keep, send):
        recv = partner(send, 1)
        ends = call(functools.partial(ends_kernel, fields), half, me, keep, recv, power)
        stages = (circ // 2).bit_length() - 1
        total = []
        for stage in range(stages):
            last = stage == stages - 1
            other = partner(ends, 2 << stage)
            total, *joined = call(
                functools.partial(stage_kernel, fields, n_circ, stage, last),
                [half] if last else [half, half],
                me, ends, other, power, *total,
            )
            total = [total]
            ends = joined[0] if joined else None
        mine, send = call(functools.partial(cells_kernel, fields), [pairs, pairs], me, keep, recv, *total, cell)
        return mine, partner(send, 1)

    def operate(parts):
        return pl.pallas_call(
            lambda *refs: operator_kernel(modes, fields, *refs),
            out_shape=[struct(rows, LANES)] * 3,
            in_specs=[smem()] * 4 + [whole()] * 6,
            out_specs=[whole()] * 3,
            scratch_shapes=[
                pltpu.VMEM((NL, 2, fields, LANES), f32),
                pltpu.VMEM((rows, LANES), f32),
                pltpu.VMEM((KM, 6, COMPS * NL, LANES), f32),
                pltpu.VMEM((KM, modes, COMPS * NL, LANES), f32),
                pltpu.SMEM((KM - 1, modes * mode_blocks), jnp.int32),
            ],
            compiler_params=params(),
        )(me, row_start, pairing, coupling, sine, stiff, stiff_l, stiff_r, *parts)

    swap = [(0, 1), (1, 0)]

    keep, send = call(
        functools.partial(first_kernel, fields), [half, half], me, b, sine, scratch_shapes=[pltpu.VMEM((NL, fields, LANES), f32)]
    )
    u, own, cross = operate(round_trip(keep, send))
    recv = lax.ppermute(cross, "mode", swap)
    keep, send, v = call(
        functools.partial(next_kernel, fields),
        [half, half, struct(rows, LANES)],
        me, b, own, recv, sine,
        scratch_shapes=[pltpu.VMEM((rows, LANES), f32), pltpu.VMEM((NL, fields, LANES), f32)],
    )
    z, own, cross = operate(round_trip(keep, send))
    recv = lax.ppermute(cross, "mode", swap)
    devices = circ * mode_blocks
    q, part = pl.pallas_call(
        lambda *refs: sums_kernel(rows, *refs),
        out_shape=[struct(rows, LANES), struct(devices, 8, LANES)],
        in_specs=[whole()] * 6,
        out_specs=[whole()] * 2,
        compiler_params=params(),
    )(b, u, v, z, own, recv)
    parts = lax.all_to_all(part, ("circ", "mode"), split_axis=0, concat_axis=0)
    x, r = pl.pallas_call(
        final_kernel,
        out_shape=[struct(rows, LANES)] * 2,
        in_specs=[whole()] * 6,
        out_specs=[whole()] * 2,
        compiler_params=params(),
    )(parts, b, u, v, z, q)

    def give(values):
        values = values[: modes * comps * NL].reshape(modes * comps, NL, local_circ, NT)
        return jnp.swapaxes(values, 1, 2).reshape(right_side.shape)

    return give(x), give(r)


def solution(mesh):
    placed = (P("mode", None, "circ", None), P(None, "circ", None), P(), P())
    return jax.shard_map(
        on_device,
        mesh=mesh,
        in_specs=placed,
        out_specs=(P("mode", None, "circ", None), P("mode", None, "circ", None)),
        check_vma=False,
    )
```

```python
import functools
import math

import jax
import jax.numpy as jnp
import numpy as np
from jax import lax
from jax.experimental import pallas as pl
from jax.experimental.pallas import tpu as pltpu
from jax.sharding import PartitionSpec as P

KM = 4
NL = 16
NT = 64
COMPS = 3
LANES = 2 * NT
HALF = NL // 2
WAYS = 2 * (KM - 1)
HIGHEST = lax.Precision.HIGHEST
F32 = jnp.float32

SHIFT = 2.0 / 3.0


def weight(comp, direction):
    return 2.0 if comp == direction else 1.0


def cosine_np():
    l = np.arange(NL)
    return np.cos(math.pi * l[None, :] * (2 * l[:, None] + 1) / (2 * NL))


COS = cosine_np()


def sine_pair():
    t = np.arange(NT) + 1
    both = np.zeros((LANES, LANES))
    both[:NT, :NT] = both[NT:, NT:] = np.sin(math.pi * t[:, None] * t[None, :] / (NT + 1))
    return both.astype(np.float32)


def root_np(comp):
    lam_l = 2.0 - 2.0 * np.cos(math.pi / NL * np.arange(NL))[:, None]
    lam_t = 2.0 - 2.0 * np.cos(math.pi / (NT + 1) * (np.arange(NT) + 1))[None, :]
    norm = np.where(np.arange(NL) == 0, 1.0 * NL, 0.5 * NL)[:, None] * (0.5 * (NT + 1))
    w = weight(comp, 0)
    half = 1.0 + (weight(comp, 1) * lam_l + weight(comp, 2) * lam_t) / (2.0 * w)
    big = half + np.sqrt(half * half - 1.0)
    return 1.0 / big, 1.0 / (w * (big - 1.0 / big) * norm)


def by_core(table):
    table = table.reshape(table.shape[0], 2, HALF, LANES)
    return np.moveaxis(table, 1, 0).astype(np.float32)


def power_table(comp, n_circ):
    root, _ = root_np(comp)
    powers = root[None] ** np.arange(n_circ - 6)[:, None, None]
    return by_core(np.concatenate([powers, powers], -1))


def cell_table(comp, n_circ):
    root, scale = root_np(comp)
    scale = scale / (1.0 - root**n_circ)

    def kernel(d):
        return scale * (root ** abs(d) + root ** (n_circ - abs(d)))

    out = []
    for low, high in ((0, 1), (2, 3), (4, -1)):
        for first, second in ((0, 1), (1, 0), (2, 3), (3, 2)):
            out.append(np.concatenate([kernel(low - first), kernel(high - second)], -1))
        out.append(np.concatenate([scale * root ** (3.0 - low), scale * root ** float(high)], -1))
        out.append(np.concatenate([scale * root ** float(low), scale * root ** (3.0 - high)], -1))
    return by_core(np.stack(out))


def low_lanes(rows):
    return lax.broadcasted_iota(jnp.int32, (rows, LANES), 1) < NT


def swap_halves(x):
    return pltpu.roll(x, NT, x.ndim - 1)


def exchange_bits(x):
    rows = x.shape[0]
    even = lax.broadcasted_iota(jnp.int32, x.shape, 0) % 2 == 0
    low = low_lanes(rows)
    other = swap_halves(x)
    moved = jnp.where(even, pltpu.roll(other, rows - 1, 0), pltpu.roll(other, 1, 0))
    return jnp.where(low == even, x, moved)


def forward(modes, core, src_ref, sine_ref, keep_ref, send_ref, rows_ref):
    plus, minus = [], []
    for l in range(HALF):
        a = src_ref[pl.ds(l, modes, stride=NL), :]
        b = src_ref[pl.ds(NL - 1 - l, modes, stride=NL), :]
        plus.append(a + b)
        minus.append(a - b)
    for m in range(NL):
        src = plus if m % 2 == 0 else minus
        acc = src[0] * float(COS[0, m])
        for l in range(1, HALF):
            acc = acc + src[l] * float(COS[l, m])
        rows_ref[pl.ds(m, modes, stride=NL), :] = acc
    rows_ref[...] = jnp.dot(rows_ref[...], sine_ref[...], precision=HIGHEST, preferred_element_type=F32)
    mine = pl.multiple_of(core * HALF, HALF)
    others = pl.multiple_of((1 - core) * HALF, HALF)
    for j in range(modes):
        keep_ref[j] = rows_ref[pl.ds(j * NL + mine, HALF), :]
        send_ref[j] = rows_ref[pl.ds(j * NL + others, HALF), :]


def first_kernel(modes, comp, me_ref, raw_ref, sine_ref, keep_ref, send_ref, b_ref, rows_ref):
    for j in range(modes):
        at = (j * COMPS + comp) * NL
        b_ref[j * NL : (j + 1) * NL, :] = exchange_bits(raw_ref[at : at + NL, :])
    forward(modes, me_ref[0] & 1, b_ref, sine_ref, keep_ref, send_ref, rows_ref)


def next_kernel(modes, me_ref, b_ref, own_ref, recv_ref, sine_ref, keep_ref, send_ref, image_ref, work_ref, rows_ref):
    image = own_ref[...] + recv_ref[...]
    image_ref[...] = image
    work_ref[...] = b_ref[...] - SHIFT * image
    forward(modes, me_ref[0] & 1, work_ref, sine_ref, keep_ref, send_ref, rows_ref)


def four_cells(core, keep, recv):
    first = jnp.where(core == 0, keep, recv)
    second = jnp.where(core == 0, recv, keep)
    return first, swap_halves(first), second, swap_halves(second)


def ends_kernel(modes, me_ref, keep_ref, recv_ref, power_ref, ends_ref):
    core = me_ref[0] & 1
    low = low_lanes(HALF)
    coefs = [
        jnp.where(low, power_ref[core, a], power_ref[core, b]) for a, b in ((0, 2), (1, 3), (2, 0), (3, 1))
    ]
    for j in range(modes):
        acc = None
        for coef, cell in zip(coefs, four_cells(core, keep_ref[j], recv_ref[j])):
            acc = coef * cell if acc is None else acc + coef * cell
        ends_ref[j] = acc


def stage_kernel(modes, n_circ, stage, last, me_ref, *refs):
    own_ref, recv_ref, power_ref = refs[:3]
    sum_ref = None if stage == 0 else refs[3]
    outs = refs[3 if stage == 0 else 4 :]
    core, chip = me_ref[0] & 1, me_ref[0] >> 1
    block = 4 << stage
    bit = (chip >> stage) & 1
    place = 4 * (chip & ((1 << stage) - 1))
    right = jnp.where(bit == 0, block - 3 - place, n_circ - 3 - place - block)
    left = jnp.where(bit == 0, n_circ - 2 * block + place + 1, place + 1)
    low = low_lanes(HALF)

    def pair(a, b):
        return jnp.where(low, power_ref[core, a], power_ref[core, b])

    action = pair(right, left)
    if not last:
        near, far = bit * block, (1 - bit) * block
        own_coef, recv_coef = pair(near, far), pair(far, near)
    for j in range(modes):
        other = recv_ref[j]
        total = action * other
        outs[0][j] = total if sum_ref is None else total + sum_ref[j]
        if not last:
            outs[1][j] = own_coef * own_ref[j] + recv_coef * other


def cells_kernel(modes, me_ref, keep_ref, recv_ref, sum_ref, cell_ref, mine_ref, send_ref):
    core = me_ref[0] & 1
    low = low_lanes(HALF)
    for j in range(modes):
        outside = sum_ref[j]
        terms = four_cells(core, keep_ref[j], recv_ref[j]) + (outside, swap_halves(outside))
        cells = []
        for group in range(3):
            acc = None
            for i, term in enumerate(terms):
                part = cell_ref[core, 6 * group + i] * term
                acc = part if acc is None else acc + part
            cells.append(acc)
        near0 = jnp.where(low, cells[1], cells[2])
        near1 = jnp.where(low, cells[2], cells[0])
        mine_ref[0, j] = jnp.where(core == 0, cells[0], cells[1])
        mine_ref[1, j] = jnp.where(core == 0, near0, near1)
        send_ref[0, j] = jnp.where(core == 0, cells[1], cells[0])
        send_ref[1, j] = jnp.where(core == 0, near1, near0)


def neighbours(mid, ends, low):
    right = swap_halves(jnp.where(low, ends, mid))
    left = swap_halves(jnp.where(low, mid, ends))
    return right, left


def lane_ends(rows):
    lane = lax.broadcasted_iota(jnp.int32, (rows, LANES), 1) % NT
    return lane == 0, lane == NT - 1


def prepare_kernel(
    modes, row_ref, pair_ref, coup_ref, own_ref, left_ref, right_ref, *refs
):
    *face_refs, index_ref, coef_ref, inv_ref = refs
    total_modes = pair_ref.shape[1]
    low = low_lanes(NL)
    first, last = lane_ends(NL)
    row = lax.broadcasted_iota(jnp.int32, (NL, LANES), 0)
    for k in range(KM):
        at = slice(k * NL, (k + 1) * NL)
        a = exchange_bits(own_ref[at, :])
        ends = jnp.where(low, exchange_bits(right_ref[at, :]), exchange_bits(left_ref[at, :]))
        right, left = neighbours(a, ends, low)
        above = jnp.where(last, a, pltpu.roll(a, LANES - 1, 1))
        below = jnp.where(first, a, pltpu.roll(a, 1, 1))
        faces = [
            0.5 * (a + right),
            0.5 * (a + left),
            jnp.where(row == NL - 1, 0.0, 0.5 * (a + pltpu.roll(a, NL - 1, 0))),
            jnp.where(row == 0, 0.0, 0.5 * (a + pltpu.roll(a, 1, 0))),
            0.5 * (a + above),
            0.5 * (a + below),
        ]
        for comp in range(COMPS):
            for nb in range(6):
                w = weight(comp, nb // 2)
                face_refs[comp][k, nb] = faces[nb] * w if w != 1.0 else faces[nb]

    def invert(j, carry):
        for k in range(KM - 1):
            inv_ref[k, pair_ref[k, j]] = j
        return carry

    lax.fori_loop(0, total_modes, invert, 0)

    def entry(i, carry):
        for k in range(KM - 1):
            for way in range(2):
                partner = pair_ref[k, i] if way == 0 else inv_ref[k, i]
                coef = 0.5 * (coup_ref[k, i] if way == 0 else coup_ref[k, partner])
                local = partner - row_ref[0]
                inside = jnp.logical_and(local >= 0, local < modes)
                coef_ref[2 * k + way, i] = jnp.where(inside, coef, 0.0)
                index_ref[2 * k + way, i] = jnp.clip(local, 0, modes - 1)
        return carry

    lax.fori_loop(0, total_modes, entry, 0)


def operator_kernel(
    modes, total_modes, me_ref, row_ref, index_ref, coef_ref, keep_ref, recv_ref, sine_ref, face_ref,
    field_ref, own_ref, cross_ref, spec_ref, ends_ref, term_ref
):
    core = me_ref[0] & 1
    mine = pl.multiple_of(core * HALF, HALF)
    others = pl.multiple_of((1 - core) * HALF, HALF)
    for part in range(2):
        for j in range(modes):
            spec_ref[part, pl.ds(j * NL + mine, HALF), :] = keep_ref[part, j]
            spec_ref[part, pl.ds(j * NL + others, HALF), :] = recv_ref[part, j]
    for part in range(2):
        spec_ref[part] = jnp.dot(spec_ref[part], sine_ref[...], precision=HIGHEST, preferred_element_type=F32)
    for part in range(2):
        dst = field_ref if part == 0 else ends_ref
        y = [spec_ref[part, pl.ds(m, modes, stride=NL), :] for m in range(NL)]
        for l in range(HALF):
            even = y[0] * float(COS[l, 0])
            odd = y[1] * float(COS[l, 1])
            for m in range(2, NL, 2):
                even = even + y[m] * float(COS[l, m])
                odd = odd + y[m + 1] * float(COS[l, m + 1])
            dst[pl.ds(l, modes, stride=NL), :] = even + odd
            dst[pl.ds(NL - 1 - l, modes, stride=NL), :] = even - odd
    low = low_lanes(NL)
    first, last = lane_ends(NL)
    for j in range(modes):
        at = slice(j * NL, (j + 1) * NL)
        mid = field_ref[at, :]
        right, left = neighbours(mid, ends_ref[at, :], low)
        diffs = [
            mid - right,
            mid - left,
            mid - pltpu.roll(mid, NL - 1, 0),
            mid - pltpu.roll(mid, 1, 0),
            mid - jnp.where(last, 0.0, pltpu.roll(mid, LANES - 1, 1)),
            mid - jnp.where(first, 0.0, pltpu.roll(mid, 1, 1)),
        ]
        for k in range(KM):
            acc = face_ref[k, 0] * diffs[0]
            for nb in range(1, 6):
                acc = acc + face_ref[k, nb] * diffs[nb]
            term_ref[k, j] = acc
    row_start = row_ref[0]
    other_start = total_modes - modes - row_start

    def mixed(i, acc):
        for e in range(WAYS):
            part = coef_ref[e, i] * term_ref[1 + e // 2, index_ref[e, i]]
            acc = part if acc is None else acc + part
        return acc

    for i in range(modes):
        cross_ref[i * NL : (i + 1) * NL, :] = mixed(other_start + i, None)
    for i in range(modes):
        own_ref[i * NL : (i + 1) * NL, :] = mixed(row_start + i, term_ref[0, i])


def sums_kernel(rows, b_ref, u_ref, v_ref, z_ref, own_ref, recv_ref, *refs):
    *before, image_ref, part_ref = refs
    q = own_ref[...] + recv_ref[...]
    image_ref[...] = q
    b, u, v, z = b_ref[...], u_ref[...], v_ref[...], z_ref[...]

    def fold(x):
        x = jnp.sum(x.reshape(rows // 8, 8, LANES), axis=0)
        return jnp.sum(x, axis=0, keepdims=True)

    sums = [fold(b * u), fold(u * v), fold(v * z), fold(b * z), fold(z * q), jnp.zeros((3, LANES), F32)]
    part = jnp.concatenate(sums, axis=0)
    part_ref[...] = part + before[0][...] if before else part


def add_kernel(a_ref, b_ref, out_ref):
    out_ref[...] = a_ref[...] + b_ref[...]


def final_kernel(modes, a_ref, b_ref, *refs):
    *fields, x_ref, r_ref = refs
    total = jnp.sum(a_ref[...] + b_ref[...], axis=1, keepdims=True)
    bu, uv, vz, bz, zq = (total[i : i + 1, :] for i in range(5))
    a0 = bu / uv
    t = vz / uv
    c1 = (bz - a0 * vz) / (zq - t * vz)
    c0 = a0 - c1 * t
    for comp in range(COMPS):
        rhs_ref, u_ref, v_ref, z_ref, q_ref = fields[5 * comp : 5 * comp + 5]
        for j in range(modes):
            at = slice(j * NL, (j + 1) * NL)
            to = (j * COMPS + comp) * NL
            x_ref[to : to + NL, :] = exchange_bits(c0 * u_ref[at, :] + c1 * z_ref[at, :])
            r_ref[to : to + NL, :] = exchange_bits(rhs_ref[at, :] - c0 * v_ref[at, :] - c1 * q_ref[at, :])


def struct(*shape, dtype=F32):
    return jax.ShapeDtypeStruct(shape, dtype)


def call(kernel, out_shape, *args, scalars=0, scalar_outs=0, scratch_shapes=()):
    vmem, smem = pl.BlockSpec(memory_space=pltpu.VMEM), pl.BlockSpec(memory_space=pltpu.SMEM)
    size = 4 * sum(math.prod(a.shape) for a in list(args) + list(out_shape))
    return pl.pallas_call(
        kernel,
        out_shape=out_shape,
        in_specs=[smem] * scalars + [vmem] * (len(args) - scalars),
        out_specs=[vmem] * (len(out_shape) - scalar_outs) + [smem] * scalar_outs,
        scratch_shapes=scratch_shapes,
        compiler_params=pltpu.CompilerParams(vmem_limit_bytes=32 * 1024 * 1024),
        cost_estimate=pl.CostEstimate(flops=4 * size, bytes_accessed=size, transcendentals=0),
    )(*args)


def on_device(right_side, stiffness, pairing, coupling):
    modes, comps, local_circ, num_cells = right_side.shape
    circ = lax.axis_size("circ")
    total_modes = pairing.shape[1]
    n_circ = local_circ * circ
    rows = modes * NL
    stages = (circ // 2).bit_length() - 1

    def raw(values, count):
        values = values.reshape(count, local_circ, num_cells // LANES, LANES)
        return jnp.swapaxes(values, 1, 2).reshape(count * NL, LANES)

    def partner(values, d):
        return lax.ppermute(values, "circ", [(i, i ^ d) for i in range(circ)])

    def other_block(values):
        return lax.ppermute(values, "mode", [(0, 1), (1, 0)])

    sine = jnp.asarray(sine_pair())
    power = [jnp.asarray(power_table(c, n_circ)) for c in range(COMPS)]
    cell = [jnp.asarray(cell_table(c, n_circ)) for c in range(COMPS)]
    row_start = (lax.axis_index("mode") * modes).astype(jnp.int32).reshape(1)
    me = lax.axis_index("circ").astype(jnp.int32).reshape(1)
    half = struct(modes, HALF, LANES)
    pairs = struct(2, modes, HALF, LANES)
    column = struct(rows, LANES)
    each = range(COMPS)

    stiff = raw(stiffness, KM)
    stiff_l = lax.ppermute(stiff, "circ", [(i, (i + 1) % circ) for i in range(circ)])
    stiff_r = lax.ppermute(stiff, "circ", [((i + 1) % circ, i) for i in range(circ)])
    *faces, index, coef = call(
        functools.partial(prepare_kernel, modes),
        [struct(KM, 6, NL, LANES)] * COMPS + [struct(WAYS, total_modes, dtype=jnp.int32), struct(WAYS, total_modes)],
        row_start, pairing, coupling, stiff, stiff_l, stiff_r,
        scalars=3, scalar_outs=2,
        scratch_shapes=[pltpu.SMEM((KM - 1, total_modes), jnp.int32)],
    )

    def round_trip(keep, send):
        recv = [partner(send[c], 1) for c in each]
        ends = [call(functools.partial(ends_kernel, modes), [half], me, keep[c], recv[c], power[c], scalars=1)[0] for c in each]
        total = [()] * COMPS
        for stage in range(stages):
            last = stage == stages - 1
            kernel = functools.partial(stage_kernel, modes, n_circ, stage, last)
            other = [partner(ends[c], 2 << stage) for c in each]
            done = [
                call(kernel, [half] if last else [half, half], me, ends[c], other[c], power[c], *total[c], scalars=1)
                for c in each
            ]
            total = [done[c][:1] for c in each]
            ends = [done[c][-1] for c in each]
        done = [
            call(functools.partial(cells_kernel, modes), [pairs, pairs], me, keep[c], recv[c], *total[c], cell[c], scalars=1)
            for c in each
        ]
        return [(done[c][0], partner(done[c][1], 1)) for c in each]

    def operate(spec):
        done = [
            call(
                functools.partial(operator_kernel, modes, total_modes),
                [column] * 3,
                me, row_start, index, coef, *spec[c], sine, faces[c],
                scalars=4,
                scratch_shapes=[
                    pltpu.VMEM((2, rows, LANES), F32),
                    pltpu.VMEM((rows, LANES), F32),
                    pltpu.VMEM((KM, modes, NL, LANES), F32),
                ],
            )
            for c in each
        ]
        field, own, cross = zip(*done)
        return field, own, [other_block(cross[c]) for c in each]

    source = raw(right_side, modes * comps)
    keep, send, b = zip(*[
        call(
            functools.partial(first_kernel, modes, c),
            [half, half, column],
            me, source, sine,
            scalars=1, scratch_shapes=[pltpu.VMEM((rows, LANES), F32)],
        )
        for c in each
    ])
    u, own, recv = operate(round_trip(keep, send))
    keep, send, v = zip(*[
        call(
            functools.partial(next_kernel, modes),
            [half, half, column],
            me, b[c], own[c], recv[c], sine,
            scalars=1, scratch_shapes=[pltpu.VMEM((rows, LANES), F32)] * 2,
        )
        for c in each
    ])
    z, own, recv = operate(round_trip(keep, send))
    q, before = [], ()
    for c in each:
        image, part = call(
            functools.partial(sums_kernel, rows), [column, struct(8, LANES)], b[c], u[c], v[c], z[c], own[c], recv[c], *before
        )
        q.append(image)
        before = (part,)
    for d in range(circ.bit_length() - 1):
        part = call(add_kernel, [struct(8, LANES)], part, partner(part, 1 << d))[0]
    other = other_block(part)
    x, r = call(
        functools.partial(final_kernel, modes),
        [struct(modes * comps * NL, LANES)] * 2,
        part, other, *[values for c in each for values in (b[c], u[c], v[c], z[c], q[c])],
    )

    def give(values):
        values = values.reshape(modes * comps, num_cells // LANES, local_circ, LANES)
        return jnp.swapaxes(values, 1, 2).reshape(right_side.shape)

    return give(x), give(r)


def solution(mesh):
    placed = (P("mode", None, "circ", None), P(None, "circ", None), P(), P())
    return jax.shard_map(
        on_device,
        mesh=mesh,
        in_specs=placed,
        out_specs=(P("mode", None, "circ", None), P("mode", None, "circ", None)),
        check_vma=False,
    )
```

```python
import functools
import math

import jax
import jax.numpy as jnp
import numpy as np
from jax import lax
from jax.experimental import pallas as pl
from jax.experimental.pallas import tpu as pltpu
from jax.sharding import PartitionSpec as P

KM = 4
NL = 16
NT = 64
COMPS = 3
LANES = 2 * NT
HALF = NL // 2
WAYS = 2 * (KM - 1)
HIGHEST = lax.Precision.HIGHEST
F32 = jnp.float32

SHIFT = 2.0 / 3.0

CHAINS = ((0,), (1, 2))


def weight(comp, direction):
    return 2.0 if comp == direction else 1.0


def cosine_np():
    l = np.arange(NL)
    return np.cos(math.pi * l[None, :] * (2 * l[:, None] + 1) / (2 * NL))


COS = cosine_np()


def sine_pair():
    t = np.arange(NT) + 1
    both = np.zeros((LANES, LANES))
    both[:NT, :NT] = both[NT:, NT:] = np.sin(math.pi * t[:, None] * t[None, :] / (NT + 1))
    return both.astype(np.float32)


def root_np(comp):
    lam_l = 2.0 - 2.0 * np.cos(math.pi / NL * np.arange(NL))[:, None]
    lam_t = 2.0 - 2.0 * np.cos(math.pi / (NT + 1) * (np.arange(NT) + 1))[None, :]
    norm = np.where(np.arange(NL) == 0, 1.0 * NL, 0.5 * NL)[:, None] * (0.5 * (NT + 1))
    w = weight(comp, 0)
    half = 1.0 + (weight(comp, 1) * lam_l + weight(comp, 2) * lam_t) / (2.0 * w)
    big = half + np.sqrt(half * half - 1.0)
    return 1.0 / big, 1.0 / (w * (big - 1.0 / big) * norm)


def by_core(table):
    table = table.reshape(table.shape[0], 2, HALF, LANES)
    return np.moveaxis(table, 1, 0).reshape(-1, LANES)


def power_table(comp, n_circ):
    root, _ = root_np(comp)
    powers = root[None] ** np.arange(n_circ - 6)[:, None, None]
    return by_core(np.concatenate([powers, powers], -1))


def cell_table(comp, n_circ):
    root, scale = root_np(comp)
    scale = scale / (1.0 - root**n_circ)

    def kernel(d):
        return scale * (root ** abs(d) + root ** (n_circ - abs(d)))

    out = []
    for low, high in ((0, 1), (2, 3), (4, -1)):
        for first, second in ((0, 1), (1, 0), (2, 3), (3, 2)):
            out.append(np.concatenate([kernel(low - first), kernel(high - second)], -1))
        out.append(np.concatenate([scale * root ** (3.0 - low), scale * root ** float(high)], -1))
        out.append(np.concatenate([scale * root ** float(low), scale * root ** (3.0 - high)], -1))
    return by_core(np.stack(out))


CELL_TERMS = 18


def all_tables(n_circ):
    parts = [sine_pair()]
    for comp in range(COMPS):
        parts += [power_table(comp, n_circ), cell_table(comp, n_circ)]
    return np.concatenate(parts).astype(np.float32)


class Tables:
    def __init__(self, ref, core, n_circ):
        self.ref, self.core, self.count = ref, core, n_circ - 6

    def sine(self):
        return self.ref[:LANES, :]

    def _tile(self, comp, offset, entry):
        base = LANES + comp * 2 * HALF * (self.count + CELL_TERMS) + offset
        return self.ref[pl.ds(pl.multiple_of(base + entry * HALF, HALF), HALF), :]

    def power(self, comp, a):
        return self._tile(comp, 0, self.core * self.count + a)

    def powers(self, comp, a, b):
        return jnp.where(low_lanes(HALF), self.power(comp, a), self.power(comp, b))

    def cell(self, comp, i):
        return self._tile(comp, 2 * HALF * self.count, self.core * CELL_TERMS + i)


def low_lanes(rows):
    return lax.broadcasted_iota(jnp.int32, (rows, LANES), 1) < NT


def swap_halves(x):
    return pltpu.roll(x, NT, x.ndim - 1)


def exchange_bits(x):
    rows = x.shape[0]
    even = lax.broadcasted_iota(jnp.int32, x.shape, 0) % 2 == 0
    low = low_lanes(rows)
    other = swap_halves(x)
    moved = jnp.where(even, pltpu.roll(other, rows - 1, 0), pltpu.roll(other, 1, 0))
    return jnp.where(low == even, x, moved)


def forward(fields, core, src_ref, sine, keep_ref, send_ref, rows_ref):
    plus, minus = [], []
    for l in range(HALF):
        a = src_ref[pl.ds(l, fields, stride=NL), :]
        b = src_ref[pl.ds(NL - 1 - l, fields, stride=NL), :]
        plus.append(a + b)
        minus.append(a - b)
    for m in range(NL):
        src = plus if m % 2 == 0 else minus
        acc = src[0] * float(COS[0, m])
        for l in range(1, HALF):
            acc = acc + src[l] * float(COS[l, m])
        rows_ref[pl.ds(m, fields, stride=NL), :] = acc
    rows_ref[...] = jnp.dot(rows_ref[...], sine, precision=HIGHEST, preferred_element_type=F32)
    mine = pl.multiple_of(core * HALF, HALF)
    others = pl.multiple_of((1 - core) * HALF, HALF)
    for j in range(fields):
        keep_ref[j] = rows_ref[pl.ds(j * NL + mine, HALF), :]
        send_ref[j] = rows_ref[pl.ds(j * NL + others, HALF), :]


def first_kernel(modes, comps, n_circ, me_ref, raw_ref, table_ref, keep_ref, send_ref, b_ref, rows_ref):
    core = me_ref[0] & 1
    for i, comp in enumerate(comps):
        for j in range(modes):
            at = (j * COMPS + comp) * NL
            to = (i * modes + j) * NL
            b_ref[to : to + NL, :] = exchange_bits(raw_ref[at : at + NL, :])
    sine = Tables(table_ref, core, n_circ).sine()
    forward(modes * len(comps), core, b_ref, sine, keep_ref, send_ref, rows_ref)


def next_kernel(
    fields, n_circ, me_ref, b_ref, own_ref, recv_ref, table_ref, keep_ref, send_ref, image_ref, work_ref, rows_ref
):
    core = me_ref[0] & 1
    image = own_ref[...] + recv_ref[...]
    image_ref[...] = image
    work_ref[...] = b_ref[...] - SHIFT * image
    forward(fields, core, work_ref, Tables(table_ref, core, n_circ).sine(), keep_ref, send_ref, rows_ref)


def four_cells(core, keep, recv):
    first = jnp.where(core == 0, keep, recv)
    second = jnp.where(core == 0, recv, keep)
    return first, swap_halves(first), second, swap_halves(second)


def ends_kernel(modes, comps, n_circ, me_ref, keep_ref, recv_ref, table_ref, ends_ref):
    core = me_ref[0] & 1
    tables = Tables(table_ref, core, n_circ)
    for i, comp in enumerate(comps):
        coefs = [tables.powers(comp, a, b) for a, b in ((0, 2), (1, 3), (2, 0), (3, 1))]
        for j in range(i * modes, (i + 1) * modes):
            acc = None
            for coef, cell in zip(coefs, four_cells(core, keep_ref[j], recv_ref[j])):
                acc = coef * cell if acc is None else acc + coef * cell
            ends_ref[j] = acc


def stage_kernel(modes, comps, n_circ, stage, last, me_ref, *refs):
    own_ref, recv_ref, table_ref = refs[:3]
    sum_ref = None if stage == 0 else refs[3]
    outs = refs[3 if stage == 0 else 4 :]
    core, chip = me_ref[0] & 1, me_ref[0] >> 1
    tables = Tables(table_ref, core, n_circ)
    block = 4 << stage
    bit = (chip >> stage) & 1
    place = 4 * (chip & ((1 << stage) - 1))
    right = jnp.where(bit == 0, block - 3 - place, n_circ - 3 - place - block)
    left = jnp.where(bit == 0, n_circ - 2 * block + place + 1, place + 1)
    near, far = bit * block, (1 - bit) * block
    for i, comp in enumerate(comps):
        action = tables.powers(comp, right, left)
        if not last:
            own_coef, recv_coef = tables.powers(comp, near, far), tables.powers(comp, far, near)
        for j in range(i * modes, (i + 1) * modes):
            other = recv_ref[j]
            total = action * other
            outs[0][j] = total if sum_ref is None else total + sum_ref[j]
            if not last:
                outs[1][j] = own_coef * own_ref[j] + recv_coef * other


def cells_kernel(modes, comps, n_circ, me_ref, keep_ref, recv_ref, sum_ref, table_ref, mine_ref, send_ref):
    core = me_ref[0] & 1
    tables = Tables(table_ref, core, n_circ)
    low = low_lanes(HALF)
    for i, comp in enumerate(comps):
        for j in range(i * modes, (i + 1) * modes):
            outside = sum_ref[j]
            terms = four_cells(core, keep_ref[j], recv_ref[j]) + (outside, swap_halves(outside))
            cells = []
            for group in range(3):
                acc = None
                for e, term in enumerate(terms):
                    part = tables.cell(comp, 6 * group + e) * term
                    acc = part if acc is None else acc + part
                cells.append(acc)
            near0 = jnp.where(low, cells[1], cells[2])
            near1 = jnp.where(low, cells[2], cells[0])
            mine_ref[0, j] = jnp.where(core == 0, cells[0], cells[1])
            mine_ref[1, j] = jnp.where(core == 0, near0, near1)
            send_ref[0, j] = jnp.where(core == 0, cells[1], cells[0])
            send_ref[1, j] = jnp.where(core == 0, near1, near0)


def neighbours(mid, ends, low):
    right = swap_halves(jnp.where(low, ends, mid))
    left = swap_halves(jnp.where(low, mid, ends))
    return right, left


def lane_ends(rows):
    lane = lax.broadcasted_iota(jnp.int32, (rows, LANES), 1) % NT
    return lane == 0, lane == NT - 1


def prepare_kernel(
    modes, row_ref, pair_ref, coup_ref, own_ref, left_ref, right_ref, *refs
):
    *face_refs, index_ref, coef_ref, inv_ref = refs
    total_modes = pair_ref.shape[1]
    low = low_lanes(NL)
    first, last = lane_ends(NL)
    row = lax.broadcasted_iota(jnp.int32, (NL, LANES), 0)
    for k in range(KM):
        at = slice(k * NL, (k + 1) * NL)
        a = exchange_bits(own_ref[at, :])
        ends = jnp.where(low, exchange_bits(right_ref[at, :]), exchange_bits(left_ref[at, :]))
        right, left = neighbours(a, ends, low)
        above = jnp.where(last, a, pltpu.roll(a, LANES - 1, 1))
        below = jnp.where(first, a, pltpu.roll(a, 1, 1))
        faces = [
            0.5 * (a + right),
            0.5 * (a + left),
            jnp.where(row == NL - 1, 0.0, 0.5 * (a + pltpu.roll(a, NL - 1, 0))),
            jnp.where(row == 0, 0.0, 0.5 * (a + pltpu.roll(a, 1, 0))),
            0.5 * (a + above),
            0.5 * (a + below),
        ]
        for comp in range(COMPS):
            for nb in range(6):
                w = weight(comp, nb // 2)
                face_refs[comp][k, nb] = faces[nb] * w if w != 1.0 else faces[nb]

    for k in range(KM - 1):
        for j in range(total_modes):
            inv_ref[k, pair_ref[k, j]] = j
    for k in range(KM - 1):
        for i in range(total_modes):
            for way in range(2):
                partner = pair_ref[k, i] if way == 0 else inv_ref[k, i]
                coef = 0.5 * (coup_ref[k, i] if way == 0 else coup_ref[k, partner])
                local = partner - row_ref[0]
                inside = jnp.logical_and(local >= 0, local < modes)
                coef_ref[2 * k + way, i] = jnp.where(inside, coef, 0.0)
                index_ref[2 * k + way, i] = jnp.clip(local, 0, modes - 1)


def operator_kernel(modes, total_modes, comps, n_circ, me_ref, row_ref, index_ref, coef_ref, keep_ref, recv_ref, table_ref, *refs):
    face_refs = refs[: len(comps)]
    field_ref, own_ref, cross_ref, spec_ref, ends_ref, term_ref = refs[len(comps) :]
    fields = modes * len(comps)
    core = me_ref[0] & 1
    sine = Tables(table_ref, core, n_circ).sine()
    mine = pl.multiple_of(core * HALF, HALF)
    others = pl.multiple_of((1 - core) * HALF, HALF)
    for part in range(2):
        for j in range(fields):
            spec_ref[part, pl.ds(j * NL + mine, HALF), :] = keep_ref[part, j]
            spec_ref[part, pl.ds(j * NL + others, HALF), :] = recv_ref[part, j]
    for part in range(2):
        spec_ref[part] = jnp.dot(spec_ref[part], sine, precision=HIGHEST, preferred_element_type=F32)
    for part in range(2):
        dst = field_ref if part == 0 else ends_ref
        y = [spec_ref[part, pl.ds(m, fields, stride=NL), :] for m in range(NL)]
        for l in range(HALF):
            even = y[0] * float(COS[l, 0])
            odd = y[1] * float(COS[l, 1])
            for m in range(2, NL, 2):
                even = even + y[m] * float(COS[l, m])
                odd = odd + y[m + 1] * float(COS[l, m + 1])
            dst[pl.ds(l, fields, stride=NL), :] = even + odd
            dst[pl.ds(NL - 1 - l, fields, stride=NL), :] = even - odd
    low = low_lanes(NL)
    first, last = lane_ends(NL)
    for j in range(fields):
        face_ref = face_refs[j // modes]
        at = slice(j * NL, (j + 1) * NL)
        mid = field_ref[at, :]
        right, left = neighbours(mid, ends_ref[at, :], low)
        diffs = [
            mid - right,
            mid - left,
            mid - pltpu.roll(mid, NL - 1, 0),
            mid - pltpu.roll(mid, 1, 0),
            mid - jnp.where(last, 0.0, pltpu.roll(mid, LANES - 1, 1)),
            mid - jnp.where(first, 0.0, pltpu.roll(mid, 1, 1)),
        ]
        for k in range(KM):
            acc = face_ref[k, 0] * diffs[0]
            for nb in range(1, 6):
                acc = acc + face_ref[k, nb] * diffs[nb]
            term_ref[k, j % modes, (j // modes) * NL : (j // modes + 1) * NL, :] = acc
    row_start = row_ref[0]
    other_start = total_modes - modes - row_start

    def mixed(i, acc):
        for e in range(WAYS):
            part = coef_ref[e, i] * term_ref[1 + e // 2, index_ref[e, i]]
            acc = part if acc is None else acc + part
        return acc

    def put(dst, i, value):
        for c in range(len(comps)):
            dst[(c * modes + i) * NL : (c * modes + i + 1) * NL, :] = value[c * NL : (c + 1) * NL, :]

    for i in range(modes):
        put(cross_ref, i, mixed(other_start + i, None))
    for i in range(modes):
        put(own_ref, i, mixed(row_start + i, term_ref[0, i]))


def sums_kernel(rows, b_ref, u_ref, v_ref, z_ref, own_ref, recv_ref, *refs):
    *before, image_ref, part_ref = refs
    q = own_ref[...] + recv_ref[...]
    image_ref[...] = q
    b, u, v, z = b_ref[...], u_ref[...], v_ref[...], z_ref[...]

    def fold(x):
        x = jnp.sum(x.reshape(rows // 8, 8, LANES), axis=0)
        return jnp.sum(x, axis=0, keepdims=True)

    sums = [fold(b * u), fold(u * v), fold(v * z), fold(b * z), fold(z * q), jnp.zeros((3, LANES), F32)]
    part = jnp.concatenate(sums, axis=0)
    if before:
        part = part + before[0][...]
    if part_ref.shape == part.shape:
        part_ref[...] = part
    else:
        for i in range(part_ref.shape[0]):
            part_ref[i] = part


def final_kernel(modes, chains, parts_ref, *refs):
    *fields, x_ref, r_ref = refs
    total = jnp.sum(jnp.sum(parts_ref[...], axis=0), axis=1, keepdims=True)
    bu, uv, vz, bz, zq = (total[i : i + 1, :] for i in range(5))
    a0 = bu / uv
    t = vz / uv
    c1 = (bz - a0 * vz) / (zq - t * vz)
    c0 = a0 - c1 * t
    for n, comps in enumerate(chains):
        rhs_ref, u_ref, v_ref, z_ref, q_ref = fields[5 * n : 5 * n + 5]
        for i, comp in enumerate(comps):
            for j in range(modes):
                at = slice((i * modes + j) * NL, (i * modes + j + 1) * NL)
                to = (j * COMPS + comp) * NL
                x_ref[to : to + NL, :] = exchange_bits(c0 * u_ref[at, :] + c1 * z_ref[at, :])
                r_ref[to : to + NL, :] = exchange_bits(rhs_ref[at, :] - c0 * v_ref[at, :] - c1 * q_ref[at, :])


def struct(*shape, dtype=F32):
    return jax.ShapeDtypeStruct(shape, dtype)


def call(kernel, out_shape, *args, scalars=0, scalar_outs=0, scratch_shapes=()):
    vmem, smem = pl.BlockSpec(memory_space=pltpu.VMEM), pl.BlockSpec(memory_space=pltpu.SMEM)
    size = 4 * sum(math.prod(a.shape) for a in list(args) + list(out_shape))
    return pl.pallas_call(
        kernel,
        out_shape=out_shape,
        in_specs=[smem] * scalars + [vmem] * (len(args) - scalars),
        out_specs=[vmem] * (len(out_shape) - scalar_outs) + [smem] * scalar_outs,
        scratch_shapes=scratch_shapes,
        compiler_params=pltpu.CompilerParams(vmem_limit_bytes=32 * 1024 * 1024),
        cost_estimate=pl.CostEstimate(flops=4 * size, bytes_accessed=size, transcendentals=0),
    )(*args)


def on_device(right_side, stiffness, pairing, coupling):
    modes, comps, local_circ, num_cells = right_side.shape
    circ = lax.axis_size("circ")
    total_modes = pairing.shape[1]
    n_circ = local_circ * circ
    stages = (circ // 2).bit_length() - 1

    def raw(values, count):
        values = values.reshape(count, local_circ, num_cells // LANES, LANES)
        return jnp.swapaxes(values, 1, 2).reshape(count * NL, LANES)

    def partner(values, d):
        return lax.ppermute(values, "circ", [(i, i ^ d) for i in range(circ)])

    def other_block(values):
        return lax.ppermute(values, "mode", [(0, 1), (1, 0)])

    table = jnp.asarray(all_tables(n_circ))
    row_start = (lax.axis_index("mode") * modes).astype(jnp.int32).reshape(1)
    me = lax.axis_index("circ").astype(jnp.int32).reshape(1)
    sizes = [modes * len(comps) for comps in CHAINS]
    half = [struct(size, HALF, LANES) for size in sizes]
    pairs = [struct(2, size, HALF, LANES) for size in sizes]
    column = [struct(size * NL, LANES) for size in sizes]
    each = range(len(CHAINS))

    stiff = raw(stiffness, KM)
    stiff_l = lax.ppermute(stiff, "circ", [(i, (i + 1) % circ) for i in range(circ)])
    stiff_r = lax.ppermute(stiff, "circ", [((i + 1) % circ, i) for i in range(circ)])
    *faces, index, coef = call(
        functools.partial(prepare_kernel, modes),
        [struct(KM, 6, NL, LANES)] * COMPS + [struct(WAYS, total_modes, dtype=jnp.int32), struct(WAYS, total_modes)],
        row_start, pairing, coupling, stiff, stiff_l, stiff_r,
        scalars=3, scalar_outs=2,
        scratch_shapes=[pltpu.SMEM((KM - 1, total_modes), jnp.int32)],
    )

    def round_trip(keep, send, hold=None):
        recv = [partner(send[c], 1) for c in each]
        ends = [
            call(
                functools.partial(ends_kernel, modes, CHAINS[c], n_circ), [half[c]], me, keep[c], recv[c], table, scalars=1
            )[0]
            for c in each
        ]
        total = [()] * len(CHAINS)
        for stage in range(stages):
            last = stage == stages - 1
            other = [partner(ends[c], 2 << stage) for c in each]
            if hold is not None and stage == 1:
                other[-1], hold = lax.optimization_barrier((other[-1], hold))
            done = [
                call(
                    functools.partial(stage_kernel, modes, CHAINS[c], n_circ, stage, last),
                    [half[c]] if last else [half[c]] * 2,
                    me, ends[c], other[c], table, *total[c],
                    scalars=1,
                )
                for c in each
            ]
            total = [done[c][:1] for c in each]
            ends = [done[c][-1] for c in each]
        done = [
            call(
                functools.partial(cells_kernel, modes, CHAINS[c], n_circ),
                [pairs[c]] * 2,
                me, keep[c], recv[c], *total[c], table,
                scalars=1,
            )
            for c in each
        ]
        return [(done[c][0], partner(done[c][1], 1)) for c in each], hold

    def operate(spec, index, coef, faces):
        done = [
            call(
                functools.partial(operator_kernel, modes, total_modes, CHAINS[c], n_circ),
                [column[c]] * 3,
                me, row_start, index, coef, *spec[c], table, *[faces[i] for i in CHAINS[c]],
                scalars=4,
                scratch_shapes=[
                    pltpu.VMEM((2, sizes[c] * NL, LANES), F32),
                    pltpu.VMEM((sizes[c] * NL, LANES), F32),
                    pltpu.VMEM((KM, modes, len(CHAINS[c]) * NL, LANES), F32),
                ],
            )
            for c in each
        ]
        field, own, cross = zip(*done)
        return field, own, [other_block(cross[c]) for c in each]

    source = raw(right_side, modes * comps)
    keep, send, b = zip(*[
        call(
            functools.partial(first_kernel, modes, CHAINS[c], n_circ),
            [half[c], half[c], column[c]],
            me, source, table,
            scalars=1, scratch_shapes=[pltpu.VMEM((sizes[c] * NL, LANES), F32)],
        )
        for c in each
    ])
    spec, hold = round_trip(keep, send, (index, coef, faces))
    u, own, recv = operate(spec, *hold)
    keep, send, v = zip(*[
        call(
            functools.partial(next_kernel, sizes[c], n_circ),
            [half[c], half[c], column[c]],
            me, b[c], own[c], recv[c], table,
            scalars=1, scratch_shapes=[pltpu.VMEM((sizes[c] * NL, LANES), F32)] * 2,
        )
        for c in each
    ])
    spec, _ = round_trip(keep, send)
    z, own, recv = operate(spec, *hold)
    devices = circ * lax.axis_size("mode")
    q, before = [], ()
    for c in each:
        shape = struct(devices, 8, LANES) if c == each[-1] else struct(8, LANES)
        image, part = call(
            functools.partial(sums_kernel, sizes[c] * NL), [column[c], shape], b[c], u[c], v[c], z[c], own[c], recv[c], *before
        )
        q.append(image)
        before = (part,)
    parts = lax.all_to_all(part, ("circ", "mode"), split_axis=0, concat_axis=0)
    x, r = call(
        functools.partial(final_kernel, modes, CHAINS),
        [struct(modes * comps * NL, LANES)] * 2,
        parts, *[values for c in each for values in (b[c], u[c], v[c], z[c], q[c])],
    )

    def give(values):
        values = values.reshape(modes * comps, num_cells // LANES, local_circ, LANES)
        return jnp.swapaxes(values, 1, 2).reshape(right_side.shape)

    return give(x), give(r)


def solution(mesh):
    placed = (P("mode", None, "circ", None), P(None, "circ", None), P(), P())
    return jax.shard_map(
        on_device,
        mesh=mesh,
        in_specs=placed,
        out_specs=(P("mode", None, "circ", None), P("mode", None, "circ", None)),
        check_vma=False,
    )
```

```python
import functools
import math

import jax
import jax.numpy as jnp
import numpy as np
from jax import lax
from jax.experimental import pallas as pl
from jax.experimental.pallas import tpu as pltpu
from jax.sharding import PartitionSpec as P

KM = 4
NL = 16
NT = 64
COMPS = 3
LANES = 2 * NT
HALF = NL // 2
WAYS = 2 * (KM - 1)
HIGHEST = lax.Precision.HIGHEST
F32 = jnp.float32

SHIFT = 2.0 / 3.0

CHAINS = ((1, 2), (0,))


def weight(comp, direction):
    return 2.0 if comp == direction else 1.0


def cosine_np():
    l = np.arange(NL)
    return np.cos(math.pi * l[None, :] * (2 * l[:, None] + 1) / (2 * NL))


COS = cosine_np()


def sine_pair():
    t = np.arange(NT) + 1
    both = np.zeros((LANES, LANES))
    both[:NT, :NT] = both[NT:, NT:] = np.sin(math.pi * t[:, None] * t[None, :] / (NT + 1))
    return both.astype(np.float32)


def root_np(comp):
    lam_l = 2.0 - 2.0 * np.cos(math.pi / NL * np.arange(NL))[:, None]
    lam_t = 2.0 - 2.0 * np.cos(math.pi / (NT + 1) * (np.arange(NT) + 1))[None, :]
    norm = np.where(np.arange(NL) == 0, 1.0 * NL, 0.5 * NL)[:, None] * (0.5 * (NT + 1))
    w = weight(comp, 0)
    half = 1.0 + (weight(comp, 1) * lam_l + weight(comp, 2) * lam_t) / (2.0 * w)
    big = half + np.sqrt(half * half - 1.0)
    return 1.0 / big, 1.0 / (w * (big - 1.0 / big) * norm)


def by_core(table):
    table = table.reshape(table.shape[0], 2, HALF, LANES)
    return np.moveaxis(table, 1, 0).reshape(-1, LANES)


def power_table(comp, n_circ):
    root, _ = root_np(comp)
    powers = root[None] ** np.arange(n_circ - 6)[:, None, None]
    return by_core(np.concatenate([powers, powers], -1))


def cell_table(comp, n_circ):
    root, scale = root_np(comp)
    scale = scale / (1.0 - root**n_circ)

    def kernel(d):
        return scale * (root ** abs(d) + root ** (n_circ - abs(d)))

    out = []
    for low, high in ((0, 1), (2, 3), (4, -1)):
        for first, second in ((0, 1), (1, 0), (2, 3), (3, 2)):
            out.append(np.concatenate([kernel(low - first), kernel(high - second)], -1))
        out.append(np.concatenate([scale * root ** (3.0 - low), scale * root ** float(high)], -1))
        out.append(np.concatenate([scale * root ** float(low), scale * root ** (3.0 - high)], -1))
    return by_core(np.stack(out))


CELL_TERMS = 18


def all_tables(n_circ):
    parts = [sine_pair()]
    for comp in range(COMPS):
        parts += [power_table(comp, n_circ), cell_table(comp, n_circ)]
    return np.concatenate(parts).astype(np.float32)


class Tables:
    def __init__(self, ref, core, n_circ):
        self.ref, self.core, self.count = ref, core, n_circ - 6

    def sine(self):
        return self.ref[:LANES, :]

    def _tile(self, comp, offset, entry):
        base = LANES + comp * 2 * HALF * (self.count + CELL_TERMS) + offset
        return self.ref[pl.ds(pl.multiple_of(base + entry * HALF, HALF), HALF), :]

    def power(self, comp, a):
        return self._tile(comp, 0, self.core * self.count + a)

    def powers(self, comp, a, b):
        return jnp.where(low_lanes(HALF), self.power(comp, a), self.power(comp, b))

    def cell(self, comp, i):
        return self._tile(comp, 2 * HALF * self.count, self.core * CELL_TERMS + i)


def low_lanes(rows):
    return lax.broadcasted_iota(jnp.int32, (rows, LANES), 1) < NT


def swap_halves(x):
    return pltpu.roll(x, NT, x.ndim - 1)


def exchange_bits(x):
    rows = x.shape[0]
    even = lax.broadcasted_iota(jnp.int32, x.shape, 0) % 2 == 0
    low = low_lanes(rows)
    other = swap_halves(x)
    moved = jnp.where(even, pltpu.roll(other, rows - 1, 0), pltpu.roll(other, 1, 0))
    return jnp.where(low == even, x, moved)


def forward(fields, core, src_ref, sine, keep_ref, send_ref, rows_ref):
    plus, minus = [], []
    for l in range(HALF):
        a = src_ref[pl.ds(l, fields, stride=NL), :]
        b = src_ref[pl.ds(NL - 1 - l, fields, stride=NL), :]
        plus.append(a + b)
        minus.append(a - b)
    for m in range(NL):
        src = plus if m % 2 == 0 else minus
        acc = src[0] * float(COS[0, m])
        for l in range(1, HALF):
            acc = acc + src[l] * float(COS[l, m])
        rows_ref[pl.ds(m, fields, stride=NL), :] = acc
    rows_ref[...] = jnp.dot(rows_ref[...], sine, precision=HIGHEST, preferred_element_type=F32)
    mine = pl.multiple_of(core * HALF, HALF)
    others = pl.multiple_of((1 - core) * HALF, HALF)
    for j in range(fields):
        keep_ref[j] = rows_ref[pl.ds(j * NL + mine, HALF), :]
        send_ref[j] = rows_ref[pl.ds(j * NL + others, HALF), :]


def first_kernel(modes, comps, n_circ, me_ref, raw_ref, table_ref, keep_ref, send_ref, b_ref, rows_ref):
    core = me_ref[0] & 1
    for i, comp in enumerate(comps):
        for j in range(modes):
            at = (j * COMPS + comp) * NL
            to = (i * modes + j) * NL
            b_ref[to : to + NL, :] = exchange_bits(raw_ref[at : at + NL, :])
    sine = Tables(table_ref, core, n_circ).sine()
    forward(modes * len(comps), core, b_ref, sine, keep_ref, send_ref, rows_ref)


def next_kernel(
    fields, n_circ, me_ref, b_ref, own_ref, recv_ref, table_ref, keep_ref, send_ref, image_ref, work_ref, rows_ref
):
    core = me_ref[0] & 1
    image = own_ref[...] + recv_ref[...]
    image_ref[...] = image
    work_ref[...] = b_ref[...] - SHIFT * image
    forward(fields, core, work_ref, Tables(table_ref, core, n_circ).sine(), keep_ref, send_ref, rows_ref)


def four_cells(core, keep, recv):
    first = jnp.where(core == 0, keep, recv)
    second = jnp.where(core == 0, recv, keep)
    return first, swap_halves(first), second, swap_halves(second)


def ends_kernel(modes, comps, n_circ, me_ref, keep_ref, recv_ref, table_ref, ends_ref):
    core = me_ref[0] & 1
    tables = Tables(table_ref, core, n_circ)
    for i, comp in enumerate(comps):
        coefs = [tables.powers(comp, a, b) for a, b in ((0, 2), (1, 3), (2, 0), (3, 1))]
        for j in range(i * modes, (i + 1) * modes):
            acc = None
            for coef, cell in zip(coefs, four_cells(core, keep_ref[j], recv_ref[j])):
                acc = coef * cell if acc is None else acc + coef * cell
            ends_ref[j] = acc


def stage_kernel(modes, comps, n_circ, stage, last, me_ref, *refs):
    own_ref, recv_ref, table_ref = refs[:3]
    sum_ref = None if stage == 0 else refs[3]
    outs = refs[3 if stage == 0 else 4 :]
    core, chip = me_ref[0] & 1, me_ref[0] >> 1
    tables = Tables(table_ref, core, n_circ)
    block = 4 << stage
    bit = (chip >> stage) & 1
    place = 4 * (chip & ((1 << stage) - 1))
    right = jnp.where(bit == 0, block - 3 - place, n_circ - 3 - place - block)
    left = jnp.where(bit == 0, n_circ - 2 * block + place + 1, place + 1)
    near, far = bit * block, (1 - bit) * block
    for i, comp in enumerate(comps):
        action = tables.powers(comp, right, left)
        if not last:
            own_coef, recv_coef = tables.powers(comp, near, far), tables.powers(comp, far, near)
        for j in range(i * modes, (i + 1) * modes):
            other = recv_ref[j]
            total = action * other
            outs[0][j] = total if sum_ref is None else total + sum_ref[j]
            if not last:
                outs[1][j] = own_coef * own_ref[j] + recv_coef * other


def cells_kernel(modes, comps, n_circ, me_ref, keep_ref, recv_ref, sum_ref, table_ref, mine_ref, send_ref):
    core = me_ref[0] & 1
    tables = Tables(table_ref, core, n_circ)
    low = low_lanes(HALF)
    for i, comp in enumerate(comps):
        for j in range(i * modes, (i + 1) * modes):
            outside = sum_ref[j]
            terms = four_cells(core, keep_ref[j], recv_ref[j]) + (outside, swap_halves(outside))
            cells = []
            for group in range(3):
                acc = None
                for e, term in enumerate(terms):
                    part = tables.cell(comp, 6 * group + e) * term
                    acc = part if acc is None else acc + part
                cells.append(acc)
            near0 = jnp.where(low, cells[1], cells[2])
            near1 = jnp.where(low, cells[2], cells[0])
            mine_ref[0, j] = jnp.where(core == 0, cells[0], cells[1])
            mine_ref[1, j] = jnp.where(core == 0, near0, near1)
            send_ref[0, j] = jnp.where(core == 0, cells[1], cells[0])
            send_ref[1, j] = jnp.where(core == 0, near1, near0)


def neighbours(mid, ends, low):
    right = swap_halves(jnp.where(low, ends, mid))
    left = swap_halves(jnp.where(low, mid, ends))
    return right, left


def lane_ends(rows):
    lane = lax.broadcasted_iota(jnp.int32, (rows, LANES), 1) % NT
    return lane == 0, lane == NT - 1


def prepare_kernel(
    modes, row_ref, pair_ref, coup_ref, own_ref, left_ref, right_ref, *refs
):
    *face_refs, index_ref, coef_ref, inv_ref = refs
    total_modes = pair_ref.shape[1]
    low = low_lanes(NL)
    first, last = lane_ends(NL)
    row = lax.broadcasted_iota(jnp.int32, (NL, LANES), 0)
    for k in range(KM):
        at = slice(k * NL, (k + 1) * NL)
        a = exchange_bits(own_ref[at, :])
        ends = jnp.where(low, exchange_bits(right_ref[at, :]), exchange_bits(left_ref[at, :]))
        right, left = neighbours(a, ends, low)
        above = jnp.where(last, a, pltpu.roll(a, LANES - 1, 1))
        below = jnp.where(first, a, pltpu.roll(a, 1, 1))
        faces = [
            0.5 * (a + right),
            0.5 * (a + left),
            jnp.where(row == NL - 1, 0.0, 0.5 * (a + pltpu.roll(a, NL - 1, 0))),
            jnp.where(row == 0, 0.0, 0.5 * (a + pltpu.roll(a, 1, 0))),
            0.5 * (a + above),
            0.5 * (a + below),
        ]
        for comp in range(COMPS):
            for nb in range(6):
                w = weight(comp, nb // 2)
                face_refs[comp][k, nb] = faces[nb] * w if w != 1.0 else faces[nb]

    for k in range(KM - 1):
        for j in range(total_modes):
            inv_ref[k, pair_ref[k, j]] = j
    for k in range(KM - 1):
        for i in range(total_modes):
            for way in range(2):
                partner = pair_ref[k, i] if way == 0 else inv_ref[k, i]
                coef = 0.5 * (coup_ref[k, i] if way == 0 else coup_ref[k, partner])
                local = partner - row_ref[0]
                inside = jnp.logical_and(local >= 0, local < modes)
                coef_ref[2 * k + way, i] = jnp.where(inside, coef, 0.0)
                index_ref[2 * k + way, i] = jnp.clip(local, 0, modes - 1)


def operator_kernel(modes, total_modes, comps, n_circ, me_ref, row_ref, index_ref, coef_ref, keep_ref, recv_ref, table_ref, *refs):
    face_refs = refs[: len(comps)]
    field_ref, own_ref, cross_ref, spec_ref, ends_ref, term_ref = refs[len(comps) :]
    fields = modes * len(comps)
    core = me_ref[0] & 1
    sine = Tables(table_ref, core, n_circ).sine()
    mine = pl.multiple_of(core * HALF, HALF)
    others = pl.multiple_of((1 - core) * HALF, HALF)
    for part in range(2):
        for j in range(fields):
            spec_ref[part, pl.ds(j * NL + mine, HALF), :] = keep_ref[part, j]
            spec_ref[part, pl.ds(j * NL + others, HALF), :] = recv_ref[part, j]
    for part in range(2):
        spec_ref[part] = jnp.dot(spec_ref[part], sine, precision=HIGHEST, preferred_element_type=F32)
    for part in range(2):
        dst = field_ref if part == 0 else ends_ref
        y = [spec_ref[part, pl.ds(m, fields, stride=NL), :] for m in range(NL)]
        for l in range(HALF):
            even = y[0] * float(COS[l, 0])
            odd = y[1] * float(COS[l, 1])
            for m in range(2, NL, 2):
                even = even + y[m] * float(COS[l, m])
                odd = odd + y[m + 1] * float(COS[l, m + 1])
            dst[pl.ds(l, fields, stride=NL), :] = even + odd
            dst[pl.ds(NL - 1 - l, fields, stride=NL), :] = even - odd
    low = low_lanes(NL)
    first, last = lane_ends(NL)
    for j in range(fields):
        face_ref = face_refs[j // modes]
        at = slice(j * NL, (j + 1) * NL)
        mid = field_ref[at, :]
        right, left = neighbours(mid, ends_ref[at, :], low)
        diffs = [
            mid - right,
            mid - left,
            mid - pltpu.roll(mid, NL - 1, 0),
            mid - pltpu.roll(mid, 1, 0),
            mid - jnp.where(last, 0.0, pltpu.roll(mid, LANES - 1, 1)),
            mid - jnp.where(first, 0.0, pltpu.roll(mid, 1, 1)),
        ]
        for k in range(KM):
            acc = face_ref[k, 0] * diffs[0]
            for nb in range(1, 6):
                acc = acc + face_ref[k, nb] * diffs[nb]
            term_ref[k, j % modes, (j // modes) * NL : (j // modes + 1) * NL, :] = acc
    row_start = row_ref[0]
    other_start = total_modes - modes - row_start

    def mixed(i, acc):
        for e in range(WAYS):
            part = coef_ref[e, i] * term_ref[1 + e // 2, index_ref[e, i]]
            acc = part if acc is None else acc + part
        return acc

    def put(dst, i, value):
        for c in range(len(comps)):
            dst[(c * modes + i) * NL : (c * modes + i + 1) * NL, :] = value[c * NL : (c + 1) * NL, :]

    for i in range(modes):
        put(cross_ref, i, mixed(other_start + i, None))
    for i in range(modes):
        put(own_ref, i, mixed(row_start + i, term_ref[0, i]))


def sums_kernel(rows, b_ref, u_ref, v_ref, z_ref, own_ref, recv_ref, *refs):
    *before, image_ref, part_ref = refs
    q = own_ref[...] + recv_ref[...]
    image_ref[...] = q
    b, u, v, z = b_ref[...], u_ref[...], v_ref[...], z_ref[...]

    def fold(x):
        x = jnp.sum(x.reshape(rows // 8, 8, LANES), axis=0)
        return jnp.sum(x, axis=0, keepdims=True)

    sums = [fold(b * u), fold(u * v), fold(v * z), fold(b * z), fold(z * q), jnp.zeros((3, LANES), F32)]
    part = jnp.concatenate(sums, axis=0)
    if before:
        part = part + before[0][...]
    if part_ref.shape == part.shape:
        part_ref[...] = part
    else:
        for i in range(part_ref.shape[0]):
            part_ref[i] = part


def final_kernel(modes, chains, parts_ref, *refs):
    *fields, x_ref, r_ref = refs
    total = jnp.sum(jnp.sum(parts_ref[...], axis=0), axis=1, keepdims=True)
    bu, uv, vz, bz, zq = (total[i : i + 1, :] for i in range(5))
    a0 = bu / uv
    t = vz / uv
    c1 = (bz - a0 * vz) / (zq - t * vz)
    c0 = a0 - c1 * t
    for n, comps in enumerate(chains):
        rhs_ref, u_ref, v_ref, z_ref, q_ref = fields[5 * n : 5 * n + 5]
        for i, comp in enumerate(comps):
            for j in range(modes):
                at = slice((i * modes + j) * NL, (i * modes + j + 1) * NL)
                to = (j * COMPS + comp) * NL
                x_ref[to : to + NL, :] = exchange_bits(c0 * u_ref[at, :] + c1 * z_ref[at, :])
                r_ref[to : to + NL, :] = exchange_bits(rhs_ref[at, :] - c0 * v_ref[at, :] - c1 * q_ref[at, :])


def struct(*shape, dtype=F32):
    return jax.ShapeDtypeStruct(shape, dtype)


class Sequence:
    def __init__(self):
        self.last = ()

    def __call__(self, kernel, out_shape, *args, scalars=0, scalar_outs=0, scratch_shapes=(), after=()):
        vmem, smem = pl.BlockSpec(memory_space=pltpu.VMEM), pl.BlockSpec(memory_space=pltpu.SMEM)
        size = 4 * sum(math.prod(a.shape) for a in list(args) + list(out_shape))
        count, unread = len(args), self.last + tuple(after)
        done = pl.pallas_call(
            lambda *refs: kernel(*refs[:count], *refs[count + len(unread) :]),
            out_shape=out_shape,
            in_specs=[smem] * scalars + [vmem] * (count - scalars) + [pl.BlockSpec(memory_space=pl.ANY)] * len(unread),
            out_specs=[vmem] * (len(out_shape) - scalar_outs) + [smem] * scalar_outs,
            scratch_shapes=scratch_shapes,
            compiler_params=pltpu.CompilerParams(vmem_limit_bytes=32 * 1024 * 1024),
            cost_estimate=pl.CostEstimate(flops=4 * size, bytes_accessed=size, transcendentals=0),
        )(*args, *unread)
        self.last = (done[0],)
        return done


def on_device(right_side, stiffness, pairing, coupling):
    modes, comps, local_circ, num_cells = right_side.shape
    circ = lax.axis_size("circ")
    total_modes = pairing.shape[1]
    n_circ = local_circ * circ
    stages = (circ // 2).bit_length() - 1

    def raw(values, count):
        values = values.reshape(count, local_circ, num_cells // LANES, LANES)
        return jnp.swapaxes(values, 1, 2).reshape(count * NL, LANES)

    def partner(values, d):
        return lax.ppermute(values, "circ", [(i, i ^ d) for i in range(circ)])

    def other_block(values):
        return lax.ppermute(values, "mode", [(0, 1), (1, 0)])

    call = Sequence()
    table = jnp.asarray(all_tables(n_circ))
    row_start = (lax.axis_index("mode") * modes).astype(jnp.int32).reshape(1)
    me = lax.axis_index("circ").astype(jnp.int32).reshape(1)
    sizes = [modes * len(comps) for comps in CHAINS]
    half = [struct(size, HALF, LANES) for size in sizes]
    pairs = [struct(2, size, HALF, LANES) for size in sizes]
    column = [struct(size * NL, LANES) for size in sizes]
    each = range(len(CHAINS))

    stiff = raw(stiffness, KM)
    stiff_l = lax.ppermute(stiff, "circ", [(i, (i + 1) % circ) for i in range(circ)])
    stiff_r = lax.ppermute(stiff, "circ", [((i + 1) % circ, i) for i in range(circ)])
    def prepare():
        return call(
            functools.partial(prepare_kernel, modes),
            [struct(KM, 6, NL, LANES)] * COMPS + [struct(WAYS, total_modes, dtype=jnp.int32), struct(WAYS, total_modes)],
            row_start, pairing, coupling, stiff, stiff_l, stiff_r,
            scalars=3, scalar_outs=2,
            scratch_shapes=[pltpu.SMEM((KM - 1, total_modes), jnp.int32)],
        )

    def round_trip(keep, send, between=lambda: None):
        recv = [partner(send[c], 1) for c in each]
        ends = [
            call(
                functools.partial(ends_kernel, modes, CHAINS[c], n_circ), [half[c]], me, keep[c], recv[c], table, scalars=1
            )[0]
            for c in each
        ]
        total = [()] * len(CHAINS)
        for stage in range(stages):
            last = stage == stages - 1
            other = [partner(ends[c], 2 << stage) for c in each]
            if stage == 0:
                extra = between()
            done = [
                call(
                    functools.partial(stage_kernel, modes, CHAINS[c], n_circ, stage, last),
                    [half[c]] if last else [half[c]] * 2,
                    me, ends[c], other[c], table, *total[c],
                    scalars=1,
                )
                for c in each
            ]
            total = [done[c][:1] for c in each]
            ends = [done[c][-1] for c in each]
        done = [
            call(
                functools.partial(cells_kernel, modes, CHAINS[c], n_circ),
                [pairs[c]] * 2,
                me, keep[c], recv[c], *total[c], table,
                scalars=1,
            )
            for c in each
        ]
        return [(done[c][0], partner(done[c][1], 1)) for c in each], extra

    def operate(spec, index, coef, faces):
        done = [
            call(
                functools.partial(operator_kernel, modes, total_modes, CHAINS[c], n_circ),
                [column[c]] * 3,
                me, row_start, index, coef, *spec[c], table, *[faces[i] for i in CHAINS[c]],
                scalars=4,
                scratch_shapes=[
                    pltpu.VMEM((2, sizes[c] * NL, LANES), F32),
                    pltpu.VMEM((sizes[c] * NL, LANES), F32),
                    pltpu.VMEM((KM, modes, len(CHAINS[c]) * NL, LANES), F32),
                ],
            )
            for c in each
        ]
        field, own, cross = zip(*done)
        return field, own, [other_block(cross[c]) for c in each]

    source = raw(right_side, modes * comps)
    keep, send, b = zip(*[
        call(
            functools.partial(first_kernel, modes, CHAINS[c], n_circ),
            [half[c], half[c], column[c]],
            me, source, table,
            scalars=1, scratch_shapes=[pltpu.VMEM((sizes[c] * NL, LANES), F32)],
            after=(stiff_l, stiff_r) if c == 1 else (),
        )
        for c in each
    ])
    spec, (*faces, index, coef) = round_trip(keep, send, prepare)
    u, own, recv = operate(spec, index, coef, faces)
    keep, send, v = zip(*[
        call(
            functools.partial(next_kernel, sizes[c], n_circ),
            [half[c], half[c], column[c]],
            me, b[c], own[c], recv[c], table,
            scalars=1, scratch_shapes=[pltpu.VMEM((sizes[c] * NL, LANES), F32)] * 2,
        )
        for c in each
    ])
    spec, _ = round_trip(keep, send)
    z, own, recv = operate(spec, index, coef, faces)
    devices = circ * lax.axis_size("mode")
    q, before = [], ()
    for c in each:
        shape = struct(devices, 8, LANES) if c == each[-1] else struct(8, LANES)
        image, part = call(
            functools.partial(sums_kernel, sizes[c] * NL), [column[c], shape], b[c], u[c], v[c], z[c], own[c], recv[c], *before
        )
        q.append(image)
        before = (part,)
    parts = lax.all_to_all(part, ("circ", "mode"), split_axis=0, concat_axis=0)
    x, r = call(
        functools.partial(final_kernel, modes, CHAINS),
        [struct(modes * comps * NL, LANES)] * 2,
        parts, *[values for c in each for values in (b[c], u[c], v[c], z[c], q[c])],
    )

    def give(values):
        values = values.reshape(modes * comps, num_cells // LANES, local_circ, LANES)
        return jnp.swapaxes(values, 1, 2).reshape(right_side.shape)

    return give(x), give(r)


def solution(mesh):
    placed = (P("mode", None, "circ", None), P(None, "circ", None), P(), P())
    return jax.shard_map(
        on_device,
        mesh=mesh,
        in_specs=placed,
        out_specs=(P("mode", None, "circ", None), P("mode", None, "circ", None)),
        check_vma=False,
    )
```
